32 devices in a mesh: energy: 8 (over y, x, core), chain: 4 (over z).
Axes of the slice: x: 2, y: 2, z: 4, core: 2. Of those that a mesh axis runs over, the one named last changes fastest.
Arguments:
- onsite: float32 [4, 2, 128, 128], P('chain'), may hold values from -0.5 to 0.5
- coupling: float32 [4, 2, 128, 128], P('chain'), may hold values from -0.3125 to 0.3125
- retained: int32 [4, 8192], P('chain'), may hold values from 0 to 16383
Outputs:
- polarization: float32 [2, 8, 4, 8192], P(None, None, 'chain', 'energy')
The draws below stay inside these ranges and needn't reach their ends.
All inputs are finite; a program needn't handle non-finite values.
Results may differ from the reference program's by a relative error of at most 0.0003.
Values sent between devices are 32-bit elements; how exact they have to be, the bound alone decides.
A program may use at most 64 MiB of HBM per device.

```python
import math
import jax
import jax.numpy as jnp
from jax import lax

ORB = 128
NK = 8192
NE = 8
NB = 4


def touch_ends(result, rng, smallest, high):
    place = [jax.random.randint(jax.random.fold_in(rng, axis), (), 0, length) for axis, length in enumerate(result.shape)]
    widest = result.shape.index(max(result.shape))
    beside = place[:widest] + [(place[widest] + 1) % result.shape[widest]] + place[widest + 1:]
    return result.at[tuple(place)].set(smallest).at[tuple(beside)].set(high)


def shard_levels(own_key, dims, shards, smallest, largest):
    def one(dim, shards_of):
        draws = jax.random.uniform(jax.random.fold_in(jax.random.fold_in(own_key, 6), dim), (shards_of,), jnp.float32, smallest / len(shards), largest / len(shards))
        return jnp.repeat(jnp.exp(draws), dims[dim] // shards_of).reshape((-1,) + (1,) * (len(dims) - dim - 1))

    gain = one(*shards[0])
    for cut in shards[1:]:
        gain = gain * one(*cut)
    return gain


def centred(key, dims, scale, limit, split=(), held_as=jnp.bfloat16):
    array = jax.random.normal(key, dims, jnp.float32) * scale
    if len(split) > 0:
        array = shard_levels(key, dims, split, -0.22, 0.18) * array
    return jnp.clip(array, min=-limit, max=limit).astype(held_as)


def setup_inputs(seed: int = 0) -> dict:
    arg_keys = jax.random.split(jax.random.key(seed), 4)
    onsite = centred(arg_keys[0], (NB, 2, ORB, ORB), ORB ** -0.5, 0.5, ((0, 4),), jnp.float32)
    coupling = centred(arg_keys[1], (NB, 2, ORB, ORB), (3 * ORB) ** -0.5, 0.3125, ((0, 4),), jnp.float32)
    retained = touch_ends(jax.random.randint(arg_keys[2], (NB, NK), 0, ORB * ORB), jax.random.fold_in(arg_keys[2], 1), 0, (ORB * ORB) - 1).astype(jnp.int32)
    return {"onsite": onsite, "coupling": coupling, "retained": retained}


broadening = 0.04

def product(left_part, right_part):
    return jnp.matmul(left_part, right_part, precision=lax.Precision.HIGHEST)

def represent(real_part, imag_part):
    upper_half = jnp.concatenate([real_part, -imag_part], axis=-1)
    lower_half = jnp.concatenate([imag_part, real_part], axis=-1)
    return jnp.concatenate([upper_half, lower_half], axis=-2)

def hermitian(raw_block):
    real_part = 0.5 * (raw_block[0] + raw_block[0].T)
    imag_part = 0.5 * (raw_block[1] - raw_block[1].T)
    return represent(real_part, imag_part)

def contact_term(coupler):
    orbitals = coupler.shape[0] // 2
    square = product(coupler, coupler.T)
    return represent(0.5 * square[orbitals:, :orbitals], -0.5 * square[:orbitals, :orbitals])

def dft_tables(length):
    positions = jnp.arange(length, dtype=jnp.int32)
    phases = positions[:, None] * positions[None, :] % length
    angles = phases.astype(jnp.float32) * (2.0 * math.pi / length)
    return (jnp.cos(angles), jnp.sin(angles))

def correlate(left_real, left_imag, right_real, right_imag):
    cosine_table, sine_table = dft_tables(left_real.shape[0])
    turn_real = product(cosine_table, left_real) - product(sine_table, left_imag)
    turn_imag = product(cosine_table, left_imag) + product(sine_table, left_real)
    back_real = product(cosine_table, right_real) + product(sine_table, right_imag)
    back_imag = product(cosine_table, right_imag) - product(sine_table, right_real)
    prod_real = turn_real * back_real - turn_imag * back_imag
    prod_imag = turn_real * back_imag + turn_imag * back_real
    inverse_count = 1.0 / left_real.shape[0]
    out_real = (product(cosine_table, prod_real) - product(sine_table, prod_imag)) * inverse_count
    out_imag = (product(cosine_table, prod_imag) + product(sine_table, prod_real)) * inverse_count
    return (out_real, out_imag)

def pick_pairs(full_block, chosen, orbitals):
    energy_count = full_block.shape[0]
    real_flat = full_block[:, :orbitals, :orbitals].reshape(energy_count, orbitals * orbitals)
    imag_flat = full_block[:, orbitals:, :orbitals].reshape(energy_count, orbitals * orbitals)
    mirror = chosen % orbitals * orbitals + chosen // orbitals
    return (real_flat[:, chosen], imag_flat[:, chosen], real_flat[:, mirror], imag_flat[:, mirror])

def shifted_energy(energy, identity):
    return represent(energy * identity, broadening * identity)

def reference(onsite, coupling, retained):
    orbitals = onsite.shape[-1]
    energy_count = NE
    blocks = NB
    energies = -2.0 + 4.0 * jnp.arange(energy_count, dtype=jnp.float32) / energy_count
    identity = jnp.eye(orbitals, dtype=jnp.float32)
    shifted = jax.vmap(shifted_energy, in_axes=(0, None))(energies, identity)
    unit_wide = jnp.broadcast_to(jnp.eye(2 * orbitals, dtype=jnp.float32), shifted.shape)
    sigma_block = jnp.zeros_like(shifted)
    greens = []
    for block_index in range(blocks):
        coupler = represent(coupling[block_index, 0], coupling[block_index, 1])
        matrix = shifted - hermitian(onsite[block_index]) - sigma_block
        if block_index == blocks - 1:
            matrix = matrix - contact_term(coupler)
        inverse = jnp.linalg.solve(matrix, unit_wide)
        greens.append(inverse)
        sigma_block = product(product(coupler.T, inverse), coupler)
    following = jnp.zeros_like(shifted)
    real_parts = [None] * blocks
    imag_parts = [None] * blocks
    for block_index in reversed(range(blocks)):
        coupler = represent(coupling[block_index, 0], coupling[block_index, 1])
        inverse = greens[block_index]
        left_part = product(inverse, coupler)
        right_part = product(coupler.T, inverse)
        full_block = inverse + product(product(left_part, following), right_part)
        following = full_block
        pairs = pick_pairs(full_block, retained[block_index], orbitals)
        out_real, out_imag = correlate(pairs[0], pairs[1], pairs[2], pairs[3])
        real_parts[block_index] = out_real
        imag_parts[block_index] = out_imag
    return jnp.stack([jnp.stack(real_parts, axis=1), jnp.stack(imag_parts, axis=1)])
```

```python
import functools

import jax
import jax.numpy as jnp
from jax import lax
from jax.experimental import pallas as pl
from jax.experimental.pallas import tpu as pltpu
from jax.sharding import PartitionSpec as P

MESH = pl.DeviceIdType.MESH
PANEL = 8
BROADENING = 0.04


def product(left, right):
    wide = jnp.concatenate(left, axis=1)
    real, imag = right
    tall = jnp.concatenate(
        [jnp.concatenate([real, imag], axis=1), jnp.concatenate([-imag, real], axis=1)], axis=0
    )
    both = jnp.dot(
        wide, tall, precision=lax.Precision.HIGHEST, preferred_element_type=jnp.float32
    )
    size = real.shape[1]
    return both[:, :size], both[:, size:]


def adjoint(value):
    return value[0].T, -value[1].T


def load(ref):
    return ref[0], ref[1]


def store(ref, value):
    ref[0] = value[0]
    ref[1] = value[1]


def across(value, column):
    return jnp.broadcast_to(value[:, column : column + 1], value.shape)


def down(value, row):
    return jnp.broadcast_to(value[row : row + 1, :], value.shape)


def pivot_inverse(real, imag):
    rows = lax.broadcasted_iota(jnp.int32, real.shape, 0)
    cols_r = [across(real, c) for c in range(PANEL)]
    cols_i = [across(imag, c) for c in range(PANEL)]
    for k in range(PANEL):
        pivot_r, pivot_i = down(cols_r[k], k), down(cols_i[k], k)
        scale = 1.0 / (pivot_r * pivot_r + pivot_i * pivot_i)
        inv_r, inv_i = pivot_r * scale, -pivot_i * scale
        here = rows == k
        factor_r = jnp.where(here, -1.0, cols_r[k])
        factor_i = jnp.where(here, 0.0, cols_i[k])
        f_r = factor_r * inv_r - factor_i * inv_i
        f_i = factor_r * inv_i + factor_i * inv_r
        for c in range(PANEL):
            if c == k:
                continue
            m_r, m_i = down(cols_r[c], k), down(cols_i[c], k)
            cols_r[c] = jnp.where(here, 0.0, cols_r[c]) - (f_r * m_r - f_i * m_i)
            cols_i[c] = jnp.where(here, 0.0, cols_i[c]) - (f_r * m_i + f_i * m_r)
        cols_r[k], cols_i[k] = -f_r, -f_i
    return tuple(cols_r) + tuple(cols_i)


def invert(ref):
    size = ref.shape[-1]
    count = size // PANEL
    shape = (PANEL, size)
    lanes = lax.broadcasted_iota(jnp.int32, shape, 1)
    rows = lax.broadcasted_iota(jnp.int32, shape, 0)
    low = lanes < PANEL
    unit = (lanes == rows).astype(jnp.float32)

    def turn(value):
        return pltpu.roll(value, size - PANEL, 1)

    def step(s, pivot):
        p_r, p_i = pivot[:PANEL], pivot[PANEL:]
        here = pl.ds(pl.multiple_of(s * PANEL, PANEL), PANEL)
        a_r = jnp.where(low, unit, ref[0, here, :])
        a_i = jnp.where(low, 0.0, ref[1, here, :])
        r_r, r_i = jnp.zeros(shape, jnp.float32), jnp.zeros(shape, jnp.float32)
        for c in range(PANEL):
            b_r, b_i = down(a_r, c), down(a_i, c)
            r_r = r_r + (p_r[c] * b_r - p_i[c] * b_i)
            r_i = r_i + (p_r[c] * b_i + p_i[c] * b_r)
        rb_r = [down(r_r, c) for c in range(PANEL)]
        rb_i = [down(r_i, c) for c in range(PANEL)]

        def updated(at):
            x_r, x_i = ref[0, at, :], ref[1, at, :]
            y_r, y_i = jnp.where(low, 0.0, x_r), jnp.where(low, 0.0, x_i)
            for c in range(PANEL):
                c_r, c_i = across(x_r, c), across(x_i, c)
                y_r = y_r - (c_r * rb_r[c] - c_i * rb_i[c])
                y_i = y_i - (c_r * rb_i[c] + c_i * rb_r[c])
            return turn(y_r), turn(y_i)

        following = lax.rem(s + 1, count)
        ahead = updated(pl.ds(pl.multiple_of(following * PANEL, PANEL), PANEL))
        later = pivot_inverse(*ahead)
        for i in range(count):
            at = pl.ds(i * PANEL, PANEL)
            z_r, z_i = updated(at)
            ref[0, at, :] = z_r
            ref[1, at, :] = z_i
        ref[0, here, :] = turn(r_r)
        ref[1, here, :] = turn(r_i)
        return later

    first = pivot_inverse(ref[0, pl.ds(0, PANEL), :], ref[1, pl.ds(0, PANEL), :])
    lax.fori_loop(0, count, step, first)


def kernel(
    groups, chains, onsite, coupling, retained, out,
    base, work, toward, left, prev, sigma_in, green_in, sigma_out, picked, table, received,
    u_send, u_recv, s_send, s_recv, g_send, g_recv, a_send, a_recv,
):
    size = onsite.shape[-1]
    me = lax.axis_index("energy")
    pos = lax.axis_index("chain")
    half = chains // 2
    in_left = pos < half
    depth = jnp.where(in_left, pos, chains - 1 - pos)
    inner = jnp.where(in_left, pos + 1, pos - 1)
    outer = jnp.where(in_left, pos - 1, pos + 1)
    middle = depth == half - 1
    at_edge = depth == 0

    barrier = pltpu.get_barrier_semaphore()

    def greet(energy, chain):
        pl.semaphore_signal(barrier, inc=1, device_id=(energy, chain), device_id_type=MESH)

    for t in range(1, groups):
        greet(lax.rem(me + t, groups), pos)
    greet(me, inner)

    @pl.when(jnp.logical_not(at_edge))
    def _():
        greet(me, outer)

    def copy(src, dst, send, recv, energy, chain):
        return pltpu.make_async_remote_copy(
            src_ref=src, dst_ref=dst, send_sem=send, recv_sem=recv,
            device_id=(energy, chain), device_id_type=MESH,
        )

    coupling_copy = copy(coupling, prev, u_send, u_recv, me, lax.rem(pos + 1, chains))
    slot = jnp.where(middle, 1, 0)
    sigma_copy = copy(sigma_out, sigma_in.at[slot], s_send, s_recv.at[slot], me, inner)
    green_copy = copy(work, green_in, g_send, g_recv, me, jnp.clip(outer, 0, chains - 1))

    def sigma_arrival(which):
        copy(sigma_out, sigma_in.at[which], s_send, s_recv.at[which], me, inner).wait_recv()

    diagonal = (
        lax.broadcasted_iota(jnp.int32, (size, size), 0)
        == lax.broadcasted_iota(jnp.int32, (size, size), 1)
    ).astype(jnp.float32)
    energy = -2.0 + 4.0 * me.astype(jnp.float32) / groups
    base[0] = energy * diagonal - 0.5 * (onsite[0] + onsite[0].T)
    base[1] = BROADENING * diagonal - 0.5 * (onsite[1] - onsite[1].T)

    @pl.when(pos == chains - 1)
    def _():
        coupler = load(coupling)
        square = product(coupler, adjoint(coupler))
        base[0] = base[0] - 0.5 * square[1]
        base[1] = base[1] + 0.5 * square[0]

    pl.semaphore_wait(barrier, groups + jnp.where(at_edge, 0, 1))

    sends_coupling = jnp.logical_and(pos >= half - 1, pos < chains - 1)

    @pl.when(sends_coupling)
    def _():
        coupling_copy.start()

    @pl.when(jnp.logical_not(at_edge))
    def _():
        sigma_arrival(0)
        base[...] = base[...] - sigma_in[0]

    work[...] = base[...]
    invert(work)

    @pl.when(in_left)
    def _():
        toward[...] = coupling[...]

    @pl.when(jnp.logical_not(in_left))
    def _():
        coupling_copy.wait_recv()
        store(toward, adjoint(load(prev)))

    store(left, product(load(work), load(toward)))
    store(sigma_out, product(adjoint(load(toward)), load(left)))
    sigma_copy.start()

    @pl.when(middle)
    def _():
        sigma_arrival(1)
        work[...] = base[...] - sigma_in[1]
        invert(work)

    @pl.when(jnp.logical_not(middle))
    def _():
        right = product(adjoint(load(toward)), load(work))
        green_copy.wait_recv()
        change = product(product(load(left), load(green_in)), right)
        work[0] = work[0] + change[0]
        work[1] = work[1] + change[1]

    @pl.when(jnp.logical_not(at_edge))
    def _():
        green_copy.start()

    full = load(work)
    planes = jnp.concatenate([full[0], full[1], full[0].T, full[1].T], axis=0)
    high = planes.astype(jnp.bfloat16)
    low = (planes - high.astype(jnp.float32)).astype(jnp.bfloat16)
    table[...] = jnp.concatenate([high, low], axis=1)
    columns = retained.shape[-1]
    across_rows = columns // 128

    def pick(group, target, place):
        chosen = retained[group]
        spot = lax.broadcasted_iota(jnp.int32, (size, columns), 0)
        hot = (spot == chosen % size).astype(jnp.float32).astype(jnp.bfloat16)
        keep = spot == chosen // size
        rows = jnp.dot(
            table[...], jnp.concatenate([hot, hot], axis=0), preferred_element_type=jnp.float32
        )
        for p in range(4):
            part = jnp.where(keep, rows[p * size : (p + 1) * size], 0.0)
            line = jnp.sum(part, axis=0, keepdims=True)
            for r in range(across_rows):
                target[place, p, r : r + 1, :] = line[:, r * 128 : (r + 1) * 128]

    def exchange(t):
        peer = lax.rem(me + t, groups)
        return copy(
            picked.at[peer], received.at[me], a_send.at[peer], a_recv.at[me], peer, pos
        )

    def send_step(t, carry):
        peer = lax.rem(me + t, groups)
        pick(peer, picked, peer)
        exchange(t).start()
        return carry

    lax.fori_loop(1, groups, send_step, 0)
    pick(me, received, me)

    def arrive_step(t, carry):
        source = lax.rem(me + t, groups)
        copy(
            picked.at[source], received.at[source], a_send.at[source], a_recv.at[source],
            source, pos,
        ).wait_recv()
        return carry

    lax.fori_loop(1, groups, arrive_step, 0)

    def shift_step(w, carry):
        real = jnp.zeros(out.shape[2:], jnp.float32)
        imag = jnp.zeros(out.shape[2:], jnp.float32)
        for n in range(groups):
            other = lax.rem(w + n, groups)
            a_r, a_i = received[n, 0], received[n, 1]
            b_r, b_i = received[other, 2], received[other, 3]
            real = real + (a_r * b_r - a_i * b_i)
            imag = imag + (a_r * b_i + a_i * b_r)
        out[0, w] = real
        out[1, w] = imag
        return carry

    lax.fori_loop(0, groups, shift_step, 0)

    sigma_copy.wait_send()

    @pl.when(sends_coupling)
    def _():
        coupling_copy.wait_send()

    @pl.when(jnp.logical_not(at_edge))
    def _():
        green_copy.wait_send()

    def leave_step(t, carry):
        exchange(t).wait_send()
        return carry

    lax.fori_loop(1, groups, leave_step, 0)


def shards(onsite, coupling, retained):
    size = onsite.shape[-1]
    groups = lax.axis_size("energy")
    chains = lax.axis_size("chain")
    columns = retained.shape[-1] // groups
    block = pltpu.VMEM((2, size, size), jnp.float32)
    picks = pltpu.VMEM((groups, 4, columns // 128, 128), jnp.float32)
    dma = pltpu.SemaphoreType.DMA
    result = pl.pallas_call(
        functools.partial(kernel, groups, chains),
        out_shape=jax.ShapeDtypeStruct((2, groups, columns // 128, 128), jnp.float32),
        in_specs=[pl.BlockSpec(memory_space=pltpu.VMEM)] * 3,
        out_specs=pl.BlockSpec(memory_space=pltpu.VMEM),
        scratch_shapes=[
            block, block, block, block, block,
            pltpu.VMEM((2, 2, size, size), jnp.float32), block, block,
            picks,
            pltpu.VMEM((4 * size, 2 * size), jnp.bfloat16),
            picks,
            dma(()), dma(()), dma(()), dma((2,)), dma(()), dma(()),
            dma((groups,)), dma((groups,)),
        ],
        compiler_params=pltpu.CompilerParams(
            collective_id=0, has_side_effects=True, vmem_limit_bytes=32 * 1024 * 1024
        ),
    )(onsite[0], coupling[0], retained.reshape(groups, 1, columns))
    return result.reshape(2, groups, 1, columns)


def solution(mesh):
    in_specs = (P("chain", None, None, None), P("chain", None, None, None), P("chain", None))
    out_specs = P(None, None, "chain", "energy")
    return jax.shard_map(shards, mesh=mesh, in_specs=in_specs, out_specs=out_specs, check_vma=False)
```

```python
import functools

import jax
import jax.numpy as jnp
from jax import lax
from jax.experimental import pallas as pl
from jax.experimental.pallas import tpu as pltpu
from jax.sharding import PartitionSpec as P

MESH = pl.DeviceIdType.MESH
SUB = 8
PANEL = 32
BROADENING = 0.04


def product(left, right):
    wide = jnp.concatenate(left, axis=1)
    real, imag = right
    tall = jnp.concatenate(
        [jnp.concatenate([real, imag], axis=1), jnp.concatenate([-imag, real], axis=1)], axis=0
    )
    both = jnp.dot(
        wide, tall, precision=lax.Precision.HIGHEST, preferred_element_type=jnp.float32
    )
    size = real.shape[1]
    return both[:, :size], both[:, size:]


def adjoint(value):
    return value[0].T, -value[1].T


def load(ref):
    return ref[0], ref[1]


def store(ref, value):
    ref[0] = value[0]
    ref[1] = value[1]


def across(value, column):
    return jnp.broadcast_to(value[:, column : column + 1], value.shape)


def down(value, row):
    return jnp.broadcast_to(value[row : row + 1, :], value.shape)


def split(value, terms):
    pieces = []
    for _ in range(terms):
        piece = value.astype(jnp.bfloat16)
        pieces.append(piece)
        value = value - piece.astype(jnp.float32)
    return pieces


def narrow_product(left, right):
    l0, l1, l2 = split(left, 3)
    r0, r1, r2 = split(right, 3)
    small = jnp.dot(
        jnp.concatenate([l0, l2], axis=1),
        jnp.concatenate([r2, r0], axis=0),
        preferred_element_type=jnp.float32,
    )
    large = jnp.dot(
        jnp.concatenate([l0, l0, l1, l1], axis=1),
        jnp.concatenate([r0, r1, r0, r1], axis=0),
        preferred_element_type=jnp.float32,
    )
    return large + small


def reciprocal(value):
    guess = pl.reciprocal(value, approx=True)
    return guess * (2.0 - value * guess)


def pivot_inverse(real, imag, start):
    rows = lax.broadcasted_iota(jnp.int32, real.shape, 0)
    cols_r = [across(real, start + c) for c in range(SUB)]
    cols_i = [across(imag, start + c) for c in range(SUB)]
    for k in range(SUB):
        pivot_r, pivot_i = down(cols_r[k], k), down(cols_i[k], k)
        scale = reciprocal(pivot_r * pivot_r + pivot_i * pivot_i)
        inv_r, inv_i = pivot_r * scale, -pivot_i * scale
        here = rows == k
        factor_r = jnp.where(here, -1.0, cols_r[k])
        factor_i = jnp.where(here, 0.0, cols_i[k])
        f_r = factor_r * inv_r - factor_i * inv_i
        f_i = factor_r * inv_i + factor_i * inv_r
        for c in range(SUB):
            if c == k:
                continue
            m_r, m_i = down(cols_r[c], k), down(cols_i[c], k)
            cols_r[c] = jnp.where(here, 0.0, cols_r[c]) - (f_r * m_r - f_i * m_i)
            cols_i[c] = jnp.where(here, 0.0, cols_i[c]) - (f_r * m_i + f_i * m_r)
        cols_r[k], cols_i[k] = -f_r, -f_i
    return cols_r, cols_i


def total(terms):
    while len(terms) > 1:
        terms = [
            terms[i] + terms[i + 1] if i + 1 < len(terms) else terms[i]
            for i in range(0, len(terms), 2)
        ]
    return terms[0]


def combine(left_r, left_i, right_r, right_i):
    real = total([a * c - b * d for a, b, c, d in zip(left_r, left_i, right_r, right_i)])
    imag = total([a * d + b * c for a, b, c, d in zip(left_r, left_i, right_r, right_i)])
    return real, imag


def invert(ref):
    size = ref.shape[-1]
    shape = (SUB, size)
    lanes = lax.broadcasted_iota(jnp.int32, shape, 1)
    rows = lax.broadcasted_iota(jnp.int32, shape, 0)
    subs = PANEL // SUB

    def turn(value):
        return pltpu.roll(value, size - PANEL, 1)

    def step(p, carry):
        first = p * PANEL
        strips = []
        for j in range(subs):
            at = pl.ds(pl.multiple_of(first + j * SUB, SUB), SUB)
            strips.append((ref[0, at, :], ref[1, at, :]))
        for s in range(subs):
            start = s * SUB
            inside = jnp.logical_and(lanes >= start, lanes < start + SUB)
            x_r, x_i = strips[s]
            p_r, p_i = pivot_inverse(x_r, x_i, start)
            a_r = jnp.where(inside, (lanes - start == rows).astype(jnp.float32), x_r)
            a_i = jnp.where(inside, 0.0, x_i)
            r_r, r_i = combine(
                p_r, p_i, [down(a_r, c) for c in range(SUB)], [down(a_i, c) for c in range(SUB)]
            )
            b_r = [down(r_r, c) for c in range(SUB)]
            b_i = [down(r_i, c) for c in range(SUB)]
            for t in range(1, subs):
                j = (s + t) % subs
                x_r, x_i = strips[j]
                d_r, d_i = combine(
                    [across(x_r, start + c) for c in range(SUB)],
                    [across(x_i, start + c) for c in range(SUB)],
                    b_r,
                    b_i,
                )
                strips[j] = (jnp.where(inside, 0.0, x_r) - d_r, jnp.where(inside, 0.0, x_i) - d_i)
            strips[s] = (r_r, r_i)
        p_r = turn(jnp.concatenate([strip[0] for strip in strips], axis=0))
        p_i = turn(jnp.concatenate([strip[1] for strip in strips], axis=0))
        m_r, m_i = ref[0], ref[1]
        change = narrow_product(
            jnp.concatenate([m_r[:, :PANEL], m_i[:, :PANEL]], axis=1),
            jnp.concatenate(
                [jnp.concatenate([p_r, p_i], axis=1), jnp.concatenate([-p_i, p_r], axis=1)], axis=0
            ),
        )
        beyond = lax.broadcasted_iota(jnp.int32, (size, size), 1) >= PANEL
        ref[0] = turn(jnp.where(beyond, m_r, 0.0)) - change[:, :size]
        ref[1] = turn(jnp.where(beyond, m_i, 0.0)) - change[:, size:]
        at = pl.ds(pl.multiple_of(first, PANEL), PANEL)
        ref[0, at, :] = p_r
        ref[1, at, :] = p_i
        return carry

    lax.fori_loop(0, size // PANEL, step, 0)


def kernel(
    groups, chains, onsite_in, coupling_in, retained_in, out, onsite, coupling, retained,
    base, work, toward, left, prev, sigma_in, green_in, sigma_out, picked, table, received,
    u_send, u_recv, s_send, s_recv, g_send, g_recv, a_send, a_recv, fetch,
):
    size = onsite.shape[-1]
    me = lax.axis_index("energy")
    pos = lax.axis_index("chain")
    half = chains // 2
    in_left = pos < half
    depth = jnp.where(in_left, pos, chains - 1 - pos)
    inner = jnp.where(in_left, pos + 1, pos - 1)
    outer = jnp.where(in_left, pos - 1, pos + 1)
    middle = depth == half - 1
    at_edge = depth == 0

    get_onsite = pltpu.make_async_copy(onsite_in, onsite, fetch.at[0])
    get_coupling = pltpu.make_async_copy(coupling_in, coupling, fetch.at[1])
    get_retained = pltpu.make_async_copy(retained_in, retained, fetch.at[2])
    get_onsite.start()
    get_coupling.start()
    get_retained.start()

    barrier = pltpu.get_barrier_semaphore()

    def greet(energy, chain):
        pl.semaphore_signal(barrier, inc=1, device_id=(energy, chain), device_id_type=MESH)

    for t in range(1, groups):
        greet(lax.rem(me + t, groups), pos)
    greet(me, inner)

    @pl.when(jnp.logical_not(at_edge))
    def _():
        greet(me, outer)

    def copy(src, dst, send, recv, energy, chain):
        return pltpu.make_async_remote_copy(
            src_ref=src, dst_ref=dst, send_sem=send, recv_sem=recv,
            device_id=(energy, chain), device_id_type=MESH,
        )

    coupling_copy = copy(coupling, prev, u_send, u_recv, me, lax.rem(pos + 1, chains))
    slot = jnp.where(middle, 1, 0)
    sigma_copy = copy(sigma_out, sigma_in.at[slot], s_send, s_recv.at[slot], me, inner)
    green_copy = copy(work, green_in, g_send, g_recv, me, jnp.clip(outer, 0, chains - 1))

    def sigma_arrival(which):
        copy(sigma_out, sigma_in.at[which], s_send, s_recv.at[which], me, inner).wait_recv()

    get_onsite.wait()
    diagonal = (
        lax.broadcasted_iota(jnp.int32, (size, size), 0)
        == lax.broadcasted_iota(jnp.int32, (size, size), 1)
    ).astype(jnp.float32)
    energy = -2.0 + 4.0 * me.astype(jnp.float32) / groups
    base[0] = energy * diagonal - 0.5 * (onsite[0] + onsite[0].T)
    base[1] = BROADENING * diagonal - 0.5 * (onsite[1] - onsite[1].T)

    get_coupling.wait()

    @pl.when(pos == chains - 1)
    def _():
        coupler = load(coupling)
        square = product(coupler, adjoint(coupler))
        base[0] = base[0] - 0.5 * square[1]
        base[1] = base[1] + 0.5 * square[0]

    pl.semaphore_wait(barrier, groups + jnp.where(at_edge, 0, 1))

    sends_coupling = jnp.logical_and(pos >= half - 1, pos < chains - 1)

    @pl.when(sends_coupling)
    def _():
        coupling_copy.start()

    @pl.when(jnp.logical_not(at_edge))
    def _():
        sigma_arrival(0)
        base[...] = base[...] - sigma_in[0]

    work[...] = base[...]
    invert(work)

    @pl.when(in_left)
    def _():
        toward[...] = coupling[...]

    @pl.when(jnp.logical_not(in_left))
    def _():
        coupling_copy.wait_recv()
        store(toward, adjoint(load(prev)))

    store(left, product(load(work), load(toward)))
    store(sigma_out, product(adjoint(load(toward)), load(left)))
    sigma_copy.start()

    @pl.when(middle)
    def _():
        sigma_arrival(1)
        work[...] = base[...] - sigma_in[1]
        invert(work)

    @pl.when(jnp.logical_not(middle))
    def _():
        right = product(adjoint(load(toward)), load(work))
        green_copy.wait_recv()
        change = product(product(load(left), load(green_in)), right)
        work[0] = work[0] + change[0]
        work[1] = work[1] + change[1]

    @pl.when(jnp.logical_not(at_edge))
    def _():
        green_copy.start()

    get_retained.wait()

    full = load(work)
    planes = jnp.concatenate([full[0], full[1], full[0].T, full[1].T], axis=0)
    high = planes.astype(jnp.bfloat16)
    low = (planes - high.astype(jnp.float32)).astype(jnp.bfloat16)
    table[...] = jnp.concatenate([high, low], axis=1)
    columns = retained.shape[-1]
    across_rows = columns // 128

    def pick(group, target, place):
        chosen = retained[group]
        spot = lax.broadcasted_iota(jnp.int32, (size, columns), 0)
        hot = (spot == chosen % size).astype(jnp.float32).astype(jnp.bfloat16)
        keep = spot == chosen // size
        rows = jnp.dot(
            table[...], jnp.concatenate([hot, hot], axis=0), preferred_element_type=jnp.float32
        )
        for p in range(4):
            part = jnp.where(keep, rows[p * size : (p + 1) * size], 0.0)
            line = jnp.sum(part, axis=0, keepdims=True)
            for r in range(across_rows):
                target[place, p, r : r + 1, :] = line[:, r * 128 : (r + 1) * 128]

    def exchange(t):
        peer = lax.rem(me + t, groups)
        return copy(
            picked.at[peer], received.at[me], a_send.at[peer], a_recv.at[me], peer, pos
        )

    def send_step(t, carry):
        peer = lax.rem(me + t, groups)
        pick(peer, picked, peer)
        exchange(t).start()
        return carry

    lax.fori_loop(1, groups, send_step, 0)
    pick(me, received, me)

    def arrive_step(t, carry):
        source = lax.rem(me + t, groups)
        copy(
            picked.at[source], received.at[source], a_send.at[source], a_recv.at[source],
            source, pos,
        ).wait_recv()
        return carry

    lax.fori_loop(1, groups, arrive_step, 0)

    def shift_step(w, carry):
        real = jnp.zeros(out.shape[2:], jnp.float32)
        imag = jnp.zeros(out.shape[2:], jnp.float32)
        for n in range(groups):
            other = lax.rem(w + n, groups)
            a_r, a_i = received[n, 0], received[n, 1]
            b_r, b_i = received[other, 2], received[other, 3]
            real = real + (a_r * b_r - a_i * b_i)
            imag = imag + (a_r * b_i + a_i * b_r)
        out[0, w] = real
        out[1, w] = imag
        return carry

    lax.fori_loop(0, groups, shift_step, 0)

    sigma_copy.wait_send()

    @pl.when(sends_coupling)
    def _():
        coupling_copy.wait_send()

    @pl.when(jnp.logical_not(at_edge))
    def _():
        green_copy.wait_send()

    def leave_step(t, carry):
        exchange(t).wait_send()
        return carry

    lax.fori_loop(1, groups, leave_step, 0)


def shards(onsite, coupling, retained):
    size = onsite.shape[-1]
    groups = lax.axis_size("energy")
    chains = lax.axis_size("chain")
    columns = retained.shape[-1] // groups
    block = pltpu.VMEM((2, size, size), jnp.float32)
    picks = pltpu.VMEM((groups, 4, columns // 128, 128), jnp.float32)
    dma = pltpu.SemaphoreType.DMA
    result = pl.pallas_call(
        functools.partial(kernel, groups, chains),
        out_shape=jax.ShapeDtypeStruct((2, groups, columns // 128, 128), jnp.float32),
        in_specs=[pl.BlockSpec(memory_space=pl.ANY)] * 3,
        out_specs=pl.BlockSpec(memory_space=pltpu.VMEM),
        scratch_shapes=[
            block, block, pltpu.VMEM((groups, 1, columns), jnp.int32),
            block, block, block, block, block,
            pltpu.VMEM((2, 2, size, size), jnp.float32), block, block,
            picks,
            pltpu.VMEM((4 * size, 2 * size), jnp.bfloat16),
            picks,
            dma(()), dma(()), dma(()), dma((2,)), dma(()), dma(()),
            dma((groups,)), dma((groups,)), dma((3,)),
        ],
        compiler_params=pltpu.CompilerParams(
            collective_id=0, has_side_effects=True, vmem_limit_bytes=32 * 1024 * 1024
        ),
    )(onsite[0], coupling[0], retained.reshape(groups, 1, columns))
    return result.reshape(2, groups, 1, columns)


def solution(mesh):
    in_specs = (P("chain", None, None, None), P("chain", None, None, None), P("chain", None))
    out_specs = P(None, None, "chain", "energy")
    return jax.shard_map(shards, mesh=mesh, in_specs=in_specs, out_specs=out_specs, check_vma=False)
```

```python
import functools

import jax
import jax.numpy as jnp
from jax import lax
from jax.experimental import pallas as pl
from jax.experimental.pallas import tpu as pltpu
from jax.sharding import PartitionSpec as P

MESH = pl.DeviceIdType.MESH
SUB = 8
PANEL = 32
BROADENING = 0.04


def product(left, right, exact=True):
    wide = jnp.concatenate(left, axis=1)
    real, imag = right
    tall = jnp.concatenate(
        [jnp.concatenate([real, imag], axis=1), jnp.concatenate([-imag, real], axis=1)], axis=0
    )
    if exact:
        both = jnp.dot(
            wide, tall, precision=lax.Precision.HIGHEST, preferred_element_type=jnp.float32
        )
    else:
        w0, w1 = split(wide, 2)
        t0, t1 = split(tall, 2)
        dot = functools.partial(jnp.dot, preferred_element_type=jnp.float32)
        both = dot(w0, t0) + (dot(w0, t1) + dot(w1, t0))
    size = real.shape[1]
    return both[:, :size], both[:, size:]


def adjoint(value):
    return value[0].T, -value[1].T


def load(ref):
    return ref[0], ref[1]


def store(ref, value):
    ref[0] = value[0]
    ref[1] = value[1]


def across(value, column):
    return jnp.broadcast_to(value[:, column : column + 1], value.shape)


def down(value, row):
    return jnp.broadcast_to(value[row : row + 1, :], value.shape)


def split(value, terms):
    pieces = []
    for _ in range(terms):
        piece = value.astype(jnp.bfloat16)
        pieces.append(piece)
        value = value - piece.astype(jnp.float32)
    return pieces


def narrow_product(left, right):
    l0, l1, l2 = split(left, 3)
    r0, r1, r2 = split(right, 3)
    small = jnp.dot(
        jnp.concatenate([l0, l2], axis=1),
        jnp.concatenate([r2, r0], axis=0),
        preferred_element_type=jnp.float32,
    )
    large = jnp.dot(
        jnp.concatenate([l0, l0, l1, l1], axis=1),
        jnp.concatenate([r0, r1, r0, r1], axis=0),
        preferred_element_type=jnp.float32,
    )
    return large + small


def reciprocal(value):
    guess = pl.reciprocal(value, approx=True)
    return guess * (2.0 - value * guess)


def pivot_inverse(real, imag, start):
    rows = lax.broadcasted_iota(jnp.int32, real.shape, 0)
    cols_r = [across(real, start + c) for c in range(SUB)]
    cols_i = [across(imag, start + c) for c in range(SUB)]
    for k in range(0, SUB, 2):
        a_r, a_i = down(cols_r[k], k), down(cols_i[k], k)
        b_r, b_i = down(cols_r[k + 1], k), down(cols_i[k + 1], k)
        c_r, c_i = down(cols_r[k], k + 1), down(cols_i[k], k + 1)
        d_r, d_i = down(cols_r[k + 1], k + 1), down(cols_i[k + 1], k + 1)
        det_r = (a_r * d_r - a_i * d_i) - (b_r * c_r - b_i * c_i)
        det_i = (a_r * d_i + a_i * d_r) - (b_r * c_i + b_i * c_r)
        scale = reciprocal(det_r * det_r + det_i * det_i)
        one, two = rows == k, rows == k + 1
        either = jnp.logical_or(one, two)
        e_r = jnp.where(one, -1.0, jnp.where(two, 0.0, cols_r[k]))
        e_i = jnp.where(either, 0.0, cols_i[k])
        f_r = jnp.where(two, -1.0, jnp.where(one, 0.0, cols_r[k + 1]))
        f_i = jnp.where(either, 0.0, cols_i[k + 1])
        u_r = (e_r * d_r - e_i * d_i) - (f_r * c_r - f_i * c_i)
        u_i = (e_r * d_i + e_i * d_r) - (f_r * c_i + f_i * c_r)
        v_r = (f_r * a_r - f_i * a_i) - (e_r * b_r - e_i * b_i)
        v_i = (f_r * a_i + f_i * a_r) - (e_r * b_i + e_i * b_r)
        u_r, u_i = u_r * det_r + u_i * det_i, u_i * det_r - u_r * det_i
        v_r, v_i = v_r * det_r + v_i * det_i, v_i * det_r - v_r * det_i
        for c in range(SUB):
            if c in (k, k + 1):
                continue
            m_r, m_i = down(cols_r[c], k), down(cols_i[c], k)
            n_r, n_i = down(cols_r[c], k + 1), down(cols_i[c], k + 1)
            w_r = (u_r * m_r - u_i * m_i) + (v_r * n_r - v_i * n_i)
            w_i = (u_r * m_i + u_i * m_r) + (v_r * n_i + v_i * n_r)
            cols_r[c] = jnp.where(either, 0.0, cols_r[c]) - scale * w_r
            cols_i[c] = jnp.where(either, 0.0, cols_i[c]) - scale * w_i
        cols_r[k], cols_i[k] = -scale * u_r, -scale * u_i
        cols_r[k + 1], cols_i[k + 1] = -scale * v_r, -scale * v_i
    return cols_r, cols_i


def total(terms):
    while len(terms) > 1:
        terms = [
            terms[i] + terms[i + 1] if i + 1 < len(terms) else terms[i]
            for i in range(0, len(terms), 2)
        ]
    return terms[0]


def combine(left_r, left_i, right_r, right_i):
    real = total([a * c - b * d for a, b, c, d in zip(left_r, left_i, right_r, right_i)])
    imag = total([a * d + b * c for a, b, c, d in zip(left_r, left_i, right_r, right_i)])
    return real, imag


def invert(ref):
    size = ref.shape[-1]
    shape = (SUB, size)
    lanes = lax.broadcasted_iota(jnp.int32, shape, 1)
    rows = lax.broadcasted_iota(jnp.int32, shape, 0)
    subs = PANEL // SUB

    def turn(value):
        return pltpu.roll(value, size - PANEL, 1)

    def step(p, carry):
        first = p * PANEL
        strips = []
        for j in range(subs):
            at = pl.ds(pl.multiple_of(first + j * SUB, SUB), SUB)
            strips.append((ref[0, at, :], ref[1, at, :]))
        for s in range(subs):
            start = s * SUB
            inside = jnp.logical_and(lanes >= start, lanes < start + SUB)
            x_r, x_i = strips[s]
            p_r, p_i = pivot_inverse(x_r, x_i, start)
            a_r = jnp.where(inside, (lanes - start == rows).astype(jnp.float32), x_r)
            a_i = jnp.where(inside, 0.0, x_i)
            r_r, r_i = combine(
                p_r, p_i, [down(a_r, c) for c in range(SUB)], [down(a_i, c) for c in range(SUB)]
            )
            b_r = [down(r_r, c) for c in range(SUB)]
            b_i = [down(r_i, c) for c in range(SUB)]
            for t in range(1, subs):
                j = (s + t) % subs
                x_r, x_i = strips[j]
                d_r, d_i = combine(
                    [across(x_r, start + c) for c in range(SUB)],
                    [across(x_i, start + c) for c in range(SUB)],
                    b_r,
                    b_i,
                )
                strips[j] = (jnp.where(inside, 0.0, x_r) - d_r, jnp.where(inside, 0.0, x_i) - d_i)
            strips[s] = (r_r, r_i)
        p_r = turn(jnp.concatenate([strip[0] for strip in strips], axis=0))
        p_i = turn(jnp.concatenate([strip[1] for strip in strips], axis=0))
        m_r, m_i = ref[0], ref[1]
        change = narrow_product(
            jnp.concatenate([m_r[:, :PANEL], m_i[:, :PANEL]], axis=1),
            jnp.concatenate(
                [jnp.concatenate([p_r, p_i], axis=1), jnp.concatenate([-p_i, p_r], axis=1)], axis=0
            ),
        )
        beyond = lax.broadcasted_iota(jnp.int32, (size, size), 1) >= PANEL
        ref[0] = turn(jnp.where(beyond, m_r, 0.0)) - change[:, :size]
        ref[1] = turn(jnp.where(beyond, m_i, 0.0)) - change[:, size:]
        at = pl.ds(pl.multiple_of(first, PANEL), PANEL)
        ref[0, at, :] = p_r
        ref[1, at, :] = p_i
        return carry

    lax.fori_loop(0, size // PANEL, step, 0)


def kernel(
    groups, chains, onsite_in, coupling_in, retained_in, out, onsite, coupling, retained,
    base, work, toward, left, prev, sigma_in, green_in, sigma_out, picked, table, received,
    u_send, u_recv, s_send, s_recv, g_send, g_recv, a_send, a_recv, fetch, hot,
):
    size = onsite.shape[-1]
    me = lax.axis_index("energy")
    pos = lax.axis_index("chain")
    half = chains // 2
    in_left = pos < half
    depth = jnp.where(in_left, pos, chains - 1 - pos)
    inner = jnp.where(in_left, pos + 1, pos - 1)
    outer = jnp.where(in_left, pos - 1, pos + 1)
    middle = depth == half - 1
    at_edge = depth == 0

    get_onsite = pltpu.make_async_copy(onsite_in, onsite, fetch.at[0])
    get_coupling = pltpu.make_async_copy(coupling_in, coupling, fetch.at[1])
    get_retained = pltpu.make_async_copy(retained_in, retained, fetch.at[2])
    get_onsite.start()
    get_coupling.start()
    get_retained.start()

    barrier = pltpu.get_barrier_semaphore()

    def greet(energy, chain):
        pl.semaphore_signal(barrier, inc=1, device_id=(energy, chain), device_id_type=MESH)

    for t in range(1, groups):
        greet(lax.rem(me + t, groups), pos)
    greet(me, inner)

    @pl.when(jnp.logical_not(at_edge))
    def _():
        greet(me, outer)

    def copy(src, dst, send, recv, energy, chain):
        return pltpu.make_async_remote_copy(
            src_ref=src, dst_ref=dst, send_sem=send, recv_sem=recv,
            device_id=(energy, chain), device_id_type=MESH,
        )

    coupling_copy = copy(coupling, prev, u_send, u_recv, me, lax.rem(pos + 1, chains))
    slot = jnp.where(middle, 1, 0)
    sigma_copy = copy(sigma_out, sigma_in.at[slot], s_send, s_recv.at[slot], me, inner)
    green_copy = copy(work, green_in, g_send, g_recv, me, jnp.clip(outer, 0, chains - 1))

    def sigma_arrival(which):
        copy(sigma_out, sigma_in.at[which], s_send, s_recv.at[which], me, inner).wait_recv()

    get_onsite.wait()
    diagonal = (
        lax.broadcasted_iota(jnp.int32, (size, size), 0)
        == lax.broadcasted_iota(jnp.int32, (size, size), 1)
    ).astype(jnp.float32)
    energy = -2.0 + 4.0 * me.astype(jnp.float32) / groups
    base[0] = energy * diagonal - 0.5 * (onsite[0] + onsite[0].T)
    base[1] = BROADENING * diagonal - 0.5 * (onsite[1] - onsite[1].T)

    get_coupling.wait()

    @pl.when(pos == chains - 1)
    def _():
        coupler = load(coupling)
        square = product(coupler, adjoint(coupler))
        base[0] = base[0] - 0.5 * square[1]
        base[1] = base[1] + 0.5 * square[0]

    @pl.when(jnp.logical_not(at_edge))
    def _():
        pl.semaphore_wait(barrier, groups + 1)


    sends_coupling = jnp.logical_and(pos >= half - 1, pos < chains - 1)

    @pl.when(sends_coupling)
    def _():
        coupling_copy.start()

    columns = retained.shape[-1]
    across_rows = columns // 128

    def prepare():
        get_retained.wait()
        spot = lax.broadcasted_iota(jnp.int32, (size, columns), 0)

        def fill(group, carry):
            one = (spot == retained[group] % size).astype(jnp.float32).astype(jnp.bfloat16)
            hot[group, pl.ds(0, size), :] = one
            hot[group, pl.ds(size, size), :] = one
            return carry

        lax.fori_loop(0, groups, fill, 0)

    @pl.when(jnp.logical_not(at_edge))
    def _():
        prepare()
        sigma_arrival(0)
        base[...] = base[...] - sigma_in[0]

    work[...] = base[...]
    invert(work)

    @pl.when(in_left)
    def _():
        toward[...] = coupling[...]

    @pl.when(jnp.logical_not(in_left))
    def _():
        coupling_copy.wait_recv()
        store(toward, adjoint(load(prev)))

    store(left, product(load(work), load(toward)))
    store(sigma_out, product(adjoint(load(toward)), load(left)))

    @pl.when(at_edge)
    def _():
        pl.semaphore_wait(barrier, groups)

    sigma_copy.start()

    @pl.when(at_edge)
    def _():
        prepare()

    @pl.when(middle)
    def _():
        sigma_arrival(1)
        work[...] = base[...] - sigma_in[1]
        invert(work)

    @pl.when(jnp.logical_not(middle))
    def _():
        right = product(adjoint(load(toward)), load(work))
        green_copy.wait_recv()
        change = product(product(load(left), load(green_in), False), right, False)
        work[0] = work[0] + change[0]
        work[1] = work[1] + change[1]

    @pl.when(jnp.logical_not(at_edge))
    def _():
        green_copy.start()

    full = load(work)
    planes = jnp.concatenate([full[0], full[1], full[0].T, full[1].T], axis=0)
    high = planes.astype(jnp.bfloat16)
    low = (planes - high.astype(jnp.float32)).astype(jnp.bfloat16)
    table[...] = jnp.concatenate([high, low], axis=1)

    def pick(group, target, place):
        chosen = retained[group]
        spot = lax.broadcasted_iota(jnp.int32, (size, columns), 0)
        keep = spot == chosen // size
        rows = jnp.dot(table[...], hot[group], preferred_element_type=jnp.float32)
        for p in range(4):
            part = jnp.where(keep, rows[p * size : (p + 1) * size], 0.0)
            line = jnp.sum(part, axis=0, keepdims=True)
            for r in range(across_rows):
                target[place, p, r : r + 1, :] = line[:, r * 128 : (r + 1) * 128]

    def exchange(t):
        peer = lax.rem(me + t, groups)
        return copy(
            picked.at[peer], received.at[me], a_send.at[peer], a_recv.at[me], peer, pos
        )

    def send_step(t, carry):
        peer = lax.rem(me + t, groups)
        pick(peer, picked, peer)
        exchange(t).start()
        return carry

    lax.fori_loop(1, groups, send_step, 0)
    pick(me, received, me)

    def arrive_step(t, carry):
        source = lax.rem(me + t, groups)
        copy(
            picked.at[source], received.at[source], a_send.at[source], a_recv.at[source],
            source, pos,
        ).wait_recv()
        return carry

    lax.fori_loop(1, groups, arrive_step, 0)

    def shift_step(w, carry):
        real = jnp.zeros(out.shape[2:], jnp.float32)
        imag = jnp.zeros(out.shape[2:], jnp.float32)
        for n in range(groups):
            other = lax.rem(w + n, groups)
            a_r, a_i = received[n, 0], received[n, 1]
            b_r, b_i = received[other, 2], received[other, 3]
            real = real + (a_r * b_r - a_i * b_i)
            imag = imag + (a_r * b_i + a_i * b_r)
        out[0, w] = real
        out[1, w] = imag
        return carry

    lax.fori_loop(0, groups, shift_step, 0)

    sigma_copy.wait_send()

    @pl.when(sends_coupling)
    def _():
        coupling_copy.wait_send()

    @pl.when(jnp.logical_not(at_edge))
    def _():
        green_copy.wait_send()

    def leave_step(t, carry):
        exchange(t).wait_send()
        return carry

    lax.fori_loop(1, groups, leave_step, 0)


def shards(onsite, coupling, retained):
    size = onsite.shape[-1]
    groups = lax.axis_size("energy")
    chains = lax.axis_size("chain")
    columns = retained.shape[-1] // groups
    block = pltpu.VMEM((2, size, size), jnp.float32)
    picks = pltpu.VMEM((groups, 4, columns // 128, 128), jnp.float32)
    dma = pltpu.SemaphoreType.DMA
    result = pl.pallas_call(
        functools.partial(kernel, groups, chains),
        out_shape=jax.ShapeDtypeStruct((2, groups, columns // 128, 128), jnp.float32),
        in_specs=[pl.BlockSpec(memory_space=pltpu.HBM)] * 3,
        out_specs=pl.BlockSpec(memory_space=pltpu.VMEM),
        scratch_shapes=[
            block, block, pltpu.VMEM((groups, 1, columns), jnp.int32),
            block, block, block, block, block,
            pltpu.VMEM((2, 2, size, size), jnp.float32), block, block,
            picks,
            pltpu.VMEM((4 * size, 2 * size), jnp.bfloat16),
            picks,
            dma(()), dma(()), dma(()), dma((2,)), dma(()), dma(()),
            dma((groups,)), dma((groups,)), dma((3,)),
            pltpu.VMEM((groups, 2 * size, columns), jnp.bfloat16),
        ],
        compiler_params=pltpu.CompilerParams(collective_id=0, has_side_effects=True),
    )(onsite[0], coupling[0], retained.reshape(groups, 1, columns))
    return result.reshape(2, groups, 1, columns)


def solution(mesh):
    in_specs = (P("chain", None, None, None), P("chain", None, None, None), P("chain", None))
    out_specs = P(None, None, "chain", "energy")
    return jax.shard_map(shards, mesh=mesh, in_specs=in_specs, out_specs=out_specs, check_vma=False)
```

```python
import functools

import jax
import jax.numpy as jnp
from jax import lax
from jax.experimental import pallas as pl
from jax.experimental.pallas import tpu as pltpu
from jax.sharding import PartitionSpec as P

MESH = pl.DeviceIdType.MESH
SUB = 8
PANEL = 32
CHUNKS = 4
GRANT = 64 * 1024 * 1024 - 80 * 1024
BROADENING = 0.04


def product(left, right, exact=True):
    wide = jnp.concatenate(left, axis=1)
    real, imag = right
    tall = jnp.concatenate(
        [jnp.concatenate([real, imag], axis=1), jnp.concatenate([-imag, real], axis=1)], axis=0
    )
    if exact:
        both = jnp.dot(
            wide, tall, precision=lax.Precision.HIGHEST, preferred_element_type=jnp.float32
        )
    else:
        w0, w1 = split(wide, 2)
        t0, t1 = split(tall, 2)
        dot = functools.partial(jnp.dot, preferred_element_type=jnp.float32)
        both = dot(w0, t0) + (dot(w0, t1) + dot(w1, t0))
    size = real.shape[1]
    return both[:, :size], both[:, size:]


def adjoint(value):
    return value[0].T, -value[1].T


def load(ref):
    return ref[0], ref[1]


def store(ref, value):
    ref[0] = value[0]
    ref[1] = value[1]


def across(value, column):
    return jnp.broadcast_to(value[:, column : column + 1], value.shape)


def down(value, row):
    return jnp.broadcast_to(value[row : row + 1, :], value.shape)


def split(value, terms):
    pieces = []
    for _ in range(terms):
        piece = value.astype(jnp.bfloat16)
        pieces.append(piece)
        value = value - piece.astype(jnp.float32)
    return pieces


def narrow_product(left, right):
    l0, l1, l2 = split(left, 3)
    r0, r1, r2 = split(right, 3)
    small = jnp.dot(
        jnp.concatenate([l0, l2], axis=1),
        jnp.concatenate([r2, r0], axis=0),
        preferred_element_type=jnp.float32,
    )
    large = jnp.dot(
        jnp.concatenate([l0, l0, l1, l1], axis=1),
        jnp.concatenate([r0, r1, r0, r1], axis=0),
        preferred_element_type=jnp.float32,
    )
    return large + small


def reciprocal(value):
    guess = pl.reciprocal(value, approx=True)
    return guess * (2.0 - value * guess)


def pivot_inverse(real, imag, start):
    rows = lax.broadcasted_iota(jnp.int32, real.shape, 0)
    cols_r = [across(real, start + c) for c in range(SUB)]
    cols_i = [across(imag, start + c) for c in range(SUB)]
    for k in range(0, SUB, 2):
        a_r, a_i = down(cols_r[k], k), down(cols_i[k], k)
        b_r, b_i = down(cols_r[k + 1], k), down(cols_i[k + 1], k)
        c_r, c_i = down(cols_r[k], k + 1), down(cols_i[k], k + 1)
        d_r, d_i = down(cols_r[k + 1], k + 1), down(cols_i[k + 1], k + 1)
        det_r = (a_r * d_r - a_i * d_i) - (b_r * c_r - b_i * c_i)
        det_i = (a_r * d_i + a_i * d_r) - (b_r * c_i + b_i * c_r)
        scale = reciprocal(det_r * det_r + det_i * det_i)
        one, two = rows == k, rows == k + 1
        either = jnp.logical_or(one, two)
        e_r = jnp.where(one, -1.0, jnp.where(two, 0.0, cols_r[k]))
        e_i = jnp.where(either, 0.0, cols_i[k])
        f_r = jnp.where(two, -1.0, jnp.where(one, 0.0, cols_r[k + 1]))
        f_i = jnp.where(either, 0.0, cols_i[k + 1])
        u_r = (e_r * d_r - e_i * d_i) - (f_r * c_r - f_i * c_i)
        u_i = (e_r * d_i + e_i * d_r) - (f_r * c_i + f_i * c_r)
        v_r = (f_r * a_r - f_i * a_i) - (e_r * b_r - e_i * b_i)
        v_i = (f_r * a_i + f_i * a_r) - (e_r * b_i + e_i * b_r)
        u_r, u_i = u_r * det_r + u_i * det_i, u_i * det_r - u_r * det_i
        v_r, v_i = v_r * det_r + v_i * det_i, v_i * det_r - v_r * det_i
        for c in range(SUB):
            if c in (k, k + 1):
                continue
            m_r, m_i = down(cols_r[c], k), down(cols_i[c], k)
            n_r, n_i = down(cols_r[c], k + 1), down(cols_i[c], k + 1)
            w_r = (u_r * m_r - u_i * m_i) + (v_r * n_r - v_i * n_i)
            w_i = (u_r * m_i + u_i * m_r) + (v_r * n_i + v_i * n_r)
            cols_r[c] = jnp.where(either, 0.0, cols_r[c]) - scale * w_r
            cols_i[c] = jnp.where(either, 0.0, cols_i[c]) - scale * w_i
        cols_r[k], cols_i[k] = -scale * u_r, -scale * u_i
        cols_r[k + 1], cols_i[k + 1] = -scale * v_r, -scale * v_i
    return cols_r, cols_i


def total(terms):
    while len(terms) > 1:
        terms = [
            terms[i] + terms[i + 1] if i + 1 < len(terms) else terms[i]
            for i in range(0, len(terms), 2)
        ]
    return terms[0]


def combine(left_r, left_i, right_r, right_i):
    real = total([a * c - b * d for a, b, c, d in zip(left_r, left_i, right_r, right_i)])
    imag = total([a * d + b * c for a, b, c, d in zip(left_r, left_i, right_r, right_i)])
    return real, imag


def invert(ref):
    size = ref.shape[-1]
    shape = (SUB, size)
    lanes = lax.broadcasted_iota(jnp.int32, shape, 1)
    rows = lax.broadcasted_iota(jnp.int32, shape, 0)
    subs = PANEL // SUB

    def turn(value):
        return pltpu.roll(value, size - PANEL, 1)

    def step(p, carry):
        first = p * PANEL
        strips = []
        for j in range(subs):
            at = pl.ds(pl.multiple_of(first + j * SUB, SUB), SUB)
            strips.append((ref[0, at, :], ref[1, at, :]))
        opening = strips[0]
        strips = [(turn(strip[0]), turn(strip[1])) for strip in strips]
        for s in range(subs):
            start = size - PANEL + s * SUB
            inside = jnp.logical_and(lanes >= start, lanes < start + SUB)
            x_r, x_i = strips[s]
            if s == 0:
                p_r, p_i = pivot_inverse(opening[0], opening[1], 0)
            else:
                p_r, p_i = pivot_inverse(x_r, x_i, start)
            a_r = jnp.where(inside, (lanes - start == rows).astype(jnp.float32), x_r)
            a_i = jnp.where(inside, 0.0, x_i)
            r_r, r_i = combine(
                p_r, p_i, [down(a_r, c) for c in range(SUB)], [down(a_i, c) for c in range(SUB)]
            )
            b_r = [down(r_r, c) for c in range(SUB)]
            b_i = [down(r_i, c) for c in range(SUB)]
            for t in range(1, subs):
                j = (s + t) % subs
                x_r, x_i = strips[j]
                d_r, d_i = combine(
                    [across(x_r, start + c) for c in range(SUB)],
                    [across(x_i, start + c) for c in range(SUB)],
                    b_r,
                    b_i,
                )
                strips[j] = (jnp.where(inside, 0.0, x_r) - d_r, jnp.where(inside, 0.0, x_i) - d_i)
            strips[s] = (r_r, r_i)
        p_r = jnp.concatenate([strip[0] for strip in strips], axis=0)
        p_i = jnp.concatenate([strip[1] for strip in strips], axis=0)
        m_r, m_i = ref[0], ref[1]
        change = narrow_product(
            jnp.concatenate([m_r[:, :PANEL], m_i[:, :PANEL]], axis=1),
            jnp.concatenate(
                [jnp.concatenate([p_r, p_i], axis=1), jnp.concatenate([-p_i, p_r], axis=1)], axis=0
            ),
        )
        beyond = lax.broadcasted_iota(jnp.int32, (size, size), 1) >= PANEL
        ref[0] = turn(jnp.where(beyond, m_r, 0.0)) - change[:, :size]
        ref[1] = turn(jnp.where(beyond, m_i, 0.0)) - change[:, size:]
        at = pl.ds(pl.multiple_of(first, PANEL), PANEL)
        ref[0, at, :] = p_r
        ref[1, at, :] = p_i
        return carry

    lax.fori_loop(0, size // PANEL, step, 0)


def kernel(
    groups, chains, onsite_in, coupling_in, retained_in, out, onsite, coupling, retained,
    base, work, toward, left, prev, sigma_in, green_in, sigma_out, picked, table, received,
    u_send, u_recv, s_send, s_recv, g_send, g_recv, a_send, a_recv, fetch, hot,
    core, ship, right, c_send, c_recv,
):
    size = onsite.shape[-1]
    me = lax.axis_index("energy")
    pos = lax.axis_index("chain")
    half = chains // 2
    in_left = pos < half
    depth = jnp.where(in_left, pos, chains - 1 - pos)
    inner = jnp.where(in_left, pos + 1, pos - 1)
    outer = jnp.where(in_left, pos - 1, pos + 1)
    middle = depth == half - 1
    at_edge = depth == 0

    get_onsite = pltpu.make_async_copy(onsite_in, onsite, fetch.at[0])
    get_coupling = pltpu.make_async_copy(coupling_in, coupling, fetch.at[1])
    get_retained = pltpu.make_async_copy(retained_in, retained, fetch.at[2])
    get_onsite.start()
    get_coupling.start()
    get_retained.start()

    barrier = pltpu.get_barrier_semaphore()

    def greet(energy, chain):
        pl.semaphore_signal(barrier, inc=1, device_id=(energy, chain), device_id_type=MESH)

    for t in range(1, groups):
        greet(lax.rem(me + t, groups), pos)
    greet(me, inner)

    @pl.when(jnp.logical_not(at_edge))
    def _():
        greet(me, outer)

    def copy(src, dst, send, recv, energy, chain):
        return pltpu.make_async_remote_copy(
            src_ref=src, dst_ref=dst, send_sem=send, recv_sem=recv,
            device_id=(energy, chain), device_id_type=MESH,
        )

    coupling_copy = copy(coupling, prev, u_send, u_recv, me, lax.rem(pos + 1, chains))
    slot = jnp.where(middle, 1, 0)
    strip = size // CHUNKS
    beyond = jnp.clip(outer, 0, chains - 1)

    def part(ref, c):
        return ref.at[:, pl.ds(c * strip, strip), :]

    def sigma_copy(which, c):
        return copy(
            part(sigma_out, c), part(sigma_in.at[which], c), s_send.at[c], s_recv.at[which, c],
            me, inner,
        )

    def core_copy(c):
        return copy(part(ship, c), part(core, c), c_send.at[c], c_recv.at[c], me, beyond)

    if half > 2:
        green_copy = copy(work, green_in, g_send, g_recv, me, beyond)
    near = depth == half - 2
    passes_on = jnp.logical_and(jnp.logical_not(at_edge), jnp.logical_not(middle))

    get_onsite.wait()
    diagonal = (
        lax.broadcasted_iota(jnp.int32, (size, size), 0)
        == lax.broadcasted_iota(jnp.int32, (size, size), 1)
    ).astype(jnp.float32)
    energy = -2.0 + 4.0 * me.astype(jnp.float32) / groups
    base[0] = energy * diagonal - 0.5 * (onsite[0] + onsite[0].T)
    base[1] = BROADENING * diagonal - 0.5 * (onsite[1] - onsite[1].T)

    get_coupling.wait()

    @pl.when(pos == chains - 1)
    def _():
        coupler = load(coupling)
        square = product(coupler, adjoint(coupler))
        base[0] = base[0] - 0.5 * square[1]
        base[1] = base[1] + 0.5 * square[0]

    @pl.when(jnp.logical_not(at_edge))
    def _():
        pl.semaphore_wait(barrier, groups + 1)


    sends_coupling = jnp.logical_and(pos >= half - 1, pos < chains - 1)

    @pl.when(sends_coupling)
    def _():
        coupling_copy.start()

    columns = retained.shape[-1]
    across_rows = columns // 128

    def prepare():
        get_retained.wait()
        spot = lax.broadcasted_iota(jnp.int32, (size, columns), 0)

        def fill(group, carry):
            one = (spot == retained[group] % size).astype(jnp.float32).astype(jnp.bfloat16)
            hot[group, pl.ds(0, size), :] = one
            hot[group, pl.ds(size, size), :] = one
            return carry

        lax.fori_loop(0, groups, fill, 0)

    @pl.when(jnp.logical_not(at_edge))
    def _():
        prepare()
        for c in range(CHUNKS):
            sigma_copy(0, c).wait_recv()
        base[...] = base[...] - sigma_in[0]

    work[...] = base[...]
    invert(work)

    @pl.when(in_left)
    def _():
        toward[...] = coupling[...]

    @pl.when(jnp.logical_not(in_left))
    def _():
        coupling_copy.wait_recv()
        store(toward, adjoint(load(prev)))

    store(left, product(load(work), load(toward)))
    store(sigma_out, product(adjoint(load(toward)), load(left)))

    @pl.when(at_edge)
    def _():
        pl.semaphore_wait(barrier, groups)

    for c in range(CHUNKS):
        sigma_copy(slot, c).start()

    @pl.when(at_edge)
    def _():
        prepare()

    @pl.when(middle)
    def _():
        for c in range(CHUNKS):
            sigma_copy(1, c).wait_recv()
            at = pl.ds(c * strip, strip)
            last = base[:, at, :] - sigma_in[1, :, at, :]
            ship[:, at, :] = last
            core_copy(c).start()
            core[:, at, :] = last

    @pl.when(jnp.logical_not(middle))
    def _():
        store(right, product(adjoint(load(toward)), load(work)))

    def add_change(following):
        change = product(product(load(left), load(following), False), load(right), False)
        work[0] = work[0] + change[0]
        work[1] = work[1] + change[1]

    @pl.when(near)
    def _():
        for c in range(CHUNKS):
            core_copy(c).wait_recv()

    @pl.when(jnp.logical_or(middle, near))
    def _():
        invert(core)

    @pl.when(middle)
    def _():
        work[...] = core[...]

    @pl.when(near)
    def _():
        add_change(core)

    if half > 2:
        @pl.when(depth < half - 2)
        def _():
            green_copy.wait_recv()
            add_change(green_in)

        @pl.when(passes_on)
        def _():
            green_copy.start()

    full = load(work)
    planes = jnp.concatenate([full[0], full[1], full[0].T, full[1].T], axis=0)
    high = planes.astype(jnp.bfloat16)
    low = (planes - high.astype(jnp.float32)).astype(jnp.bfloat16)
    table[...] = jnp.concatenate([high, low], axis=1)

    def pick(group, target, place):
        chosen = retained[group]
        spot = lax.broadcasted_iota(jnp.int32, (size, columns), 0)
        keep = spot == chosen // size
        rows = jnp.dot(table[...], hot[group], preferred_element_type=jnp.float32)
        for p in range(4):
            part = jnp.where(keep, rows[p * size : (p + 1) * size], 0.0)
            line = jnp.sum(part, axis=0, keepdims=True)
            for r in range(across_rows):
                target[place, p, r : r + 1, :] = line[:, r * 128 : (r + 1) * 128]

    def exchange(t):
        peer = lax.rem(me + t, groups)
        return copy(
            picked.at[peer], received.at[me], a_send.at[peer], a_recv.at[me], peer, pos
        )

    def send_step(t, carry):
        peer = lax.rem(me + t, groups)
        pick(peer, picked, peer)
        exchange(t).start()
        return carry

    lax.fori_loop(1, groups, send_step, 0)
    pick(me, received, me)

    def arrive_step(t, carry):
        source = lax.rem(me + t, groups)
        copy(
            picked.at[source], received.at[source], a_send.at[source], a_recv.at[source],
            source, pos,
        ).wait_recv()
        return carry

    lax.fori_loop(1, groups, arrive_step, 0)

    def shift_step(w, carry):
        real = jnp.zeros(out.shape[2:], jnp.float32)
        imag = jnp.zeros(out.shape[2:], jnp.float32)
        for n in range(groups):
            other = lax.rem(w + n, groups)
            a_r, a_i = received[n, 0], received[n, 1]
            b_r, b_i = received[other, 2], received[other, 3]
            real = real + (a_r * b_r - a_i * b_i)
            imag = imag + (a_r * b_i + a_i * b_r)
        out[0, w] = real
        out[1, w] = imag
        return carry

    lax.fori_loop(0, groups, shift_step, 0)

    for c in range(CHUNKS):
        sigma_copy(slot, c).wait_send()

    @pl.when(middle)
    def _():
        for c in range(CHUNKS):
            core_copy(c).wait_send()

    @pl.when(sends_coupling)
    def _():
        coupling_copy.wait_send()

    if half > 2:
        @pl.when(passes_on)
        def _():
            green_copy.wait_send()

    def leave_step(t, carry):
        exchange(t).wait_send()
        return carry

    lax.fori_loop(1, groups, leave_step, 0)


def shards(onsite, coupling, retained):
    size = onsite.shape[-1]
    groups = lax.axis_size("energy")
    chains = lax.axis_size("chain")
    columns = retained.shape[-1] // groups
    block = pltpu.VMEM((2, size, size), jnp.float32)
    picks = pltpu.VMEM((groups, 4, columns // 128, 128), jnp.float32)
    dma = pltpu.SemaphoreType.DMA
    result = pl.pallas_call(
        functools.partial(kernel, groups, chains),
        out_shape=jax.ShapeDtypeStruct((2, groups, columns // 128, 128), jnp.float32),
        in_specs=[pl.BlockSpec(memory_space=pltpu.HBM)] * 3,
        out_specs=pl.BlockSpec(memory_space=pltpu.VMEM),
        scratch_shapes=[
            block, block, pltpu.VMEM((groups, 1, columns), jnp.int32),
            block, block, block, block, block,
            pltpu.VMEM((2, 2, size, size), jnp.float32), block, block,
            picks,
            pltpu.VMEM((4 * size, 2 * size), jnp.bfloat16),
            picks,
            dma(()), dma(()), dma((CHUNKS,)), dma((2, CHUNKS)), dma(()), dma(()),
            dma((groups,)), dma((groups,)), dma((3,)),
            pltpu.VMEM((groups, 2 * size, columns), jnp.bfloat16),
            block, block, block, dma((CHUNKS,)), dma((CHUNKS,)),
        ],
        compiler_params=pltpu.CompilerParams(
            collective_id=0, has_side_effects=True, vmem_limit_bytes=GRANT
        ),
    )(onsite[0], coupling[0], retained.reshape(groups, 1, columns))
    return result.reshape(2, groups, 1, columns)


def solution(mesh):
    in_specs = (P("chain", None, None, None), P("chain", None, None, None), P("chain", None))
    out_specs = P(None, None, "chain", "energy")
    return jax.shard_map(shards, mesh=mesh, in_specs=in_specs, out_specs=out_specs, check_vma=False)
```

```python
import functools

import jax
import jax.numpy as jnp
from jax import lax
from jax.experimental import pallas as pl
from jax.experimental.pallas import tpu as pltpu
from jax.sharding import PartitionSpec as P

MESH = pl.DeviceIdType.MESH
SUB = 8
PANEL = 64
CHUNKS = 4
GRANT = 64 * 1024 * 1024 - 256 * 1024
BROADENING = 0.04


def product(left, right, exact=True):
    wide = jnp.concatenate(left, axis=1)
    real, imag = right
    tall = jnp.concatenate(
        [jnp.concatenate([real, imag], axis=1), jnp.concatenate([-imag, real], axis=1)], axis=0
    )
    if exact:
        both = jnp.dot(
            wide, tall, precision=lax.Precision.HIGHEST, preferred_element_type=jnp.float32
        )
    else:
        w0, w1 = split(wide, 2)
        t0, t1 = split(tall, 2)
        dot = functools.partial(jnp.dot, preferred_element_type=jnp.float32)
        both = dot(w0, t0) + (dot(w0, t1) + dot(w1, t0))
    size = real.shape[1]
    return both[:, :size], both[:, size:]


def adjoint(value):
    return value[0].T, -value[1].T


def load(ref):
    return ref[0], ref[1]


def store(ref, value):
    ref[0] = value[0]
    ref[1] = value[1]


def across(value, column):
    return jnp.broadcast_to(value[:, column : column + 1], value.shape)


def down(value, row):
    return jnp.broadcast_to(value[row : row + 1, :], value.shape)


def split(value, terms):
    pieces = []
    for _ in range(terms):
        piece = value.astype(jnp.bfloat16)
        pieces.append(piece)
        value = value - piece.astype(jnp.float32)
    return pieces


def narrow_product(left, right):
    l0, l1, l2 = split(left, 3)
    r0, r1, r2 = split(right, 3)
    small = jnp.dot(
        jnp.concatenate([l0, l2], axis=1),
        jnp.concatenate([r2, r0], axis=0),
        preferred_element_type=jnp.float32,
    )
    large = jnp.dot(
        jnp.concatenate([l0, l0, l1, l1], axis=1),
        jnp.concatenate([r0, r1, r0, r1], axis=0),
        preferred_element_type=jnp.float32,
    )
    return large + small


def reciprocal(value):
    guess = pl.reciprocal(value, approx=True)
    return guess * (2.0 - value * guess)


def pivot_inverse(real, imag, start):
    rows = lax.broadcasted_iota(jnp.int32, real.shape, 0)
    cols_r = [across(real, start + c) for c in range(SUB)]
    cols_i = [across(imag, start + c) for c in range(SUB)]
    for k in range(0, SUB, 2):
        a_r, a_i = down(cols_r[k], k), down(cols_i[k], k)
        b_r, b_i = down(cols_r[k + 1], k), down(cols_i[k + 1], k)
        c_r, c_i = down(cols_r[k], k + 1), down(cols_i[k], k + 1)
        d_r, d_i = down(cols_r[k + 1], k + 1), down(cols_i[k + 1], k + 1)
        det_r = (a_r * d_r - a_i * d_i) - (b_r * c_r - b_i * c_i)
        det_i = (a_r * d_i + a_i * d_r) - (b_r * c_i + b_i * c_r)
        scale = reciprocal(det_r * det_r + det_i * det_i)
        one, two = rows == k, rows == k + 1
        either = jnp.logical_or(one, two)
        e_r = jnp.where(one, -1.0, jnp.where(two, 0.0, cols_r[k]))
        e_i = jnp.where(either, 0.0, cols_i[k])
        f_r = jnp.where(two, -1.0, jnp.where(one, 0.0, cols_r[k + 1]))
        f_i = jnp.where(either, 0.0, cols_i[k + 1])
        u_r = (e_r * d_r - e_i * d_i) - (f_r * c_r - f_i * c_i)
        u_i = (e_r * d_i + e_i * d_r) - (f_r * c_i + f_i * c_r)
        v_r = (f_r * a_r - f_i * a_i) - (e_r * b_r - e_i * b_i)
        v_i = (f_r * a_i + f_i * a_r) - (e_r * b_i + e_i * b_r)
        u_r, u_i = u_r * det_r + u_i * det_i, u_i * det_r - u_r * det_i
        v_r, v_i = v_r * det_r + v_i * det_i, v_i * det_r - v_r * det_i
        for c in range(SUB):
            if c in (k, k + 1):
                continue
            m_r, m_i = down(cols_r[c], k), down(cols_i[c], k)
            n_r, n_i = down(cols_r[c], k + 1), down(cols_i[c], k + 1)
            w_r = (u_r * m_r - u_i * m_i) + (v_r * n_r - v_i * n_i)
            w_i = (u_r * m_i + u_i * m_r) + (v_r * n_i + v_i * n_r)
            cols_r[c] = jnp.where(either, 0.0, cols_r[c]) - scale * w_r
            cols_i[c] = jnp.where(either, 0.0, cols_i[c]) - scale * w_i
        cols_r[k], cols_i[k] = -scale * u_r, -scale * u_i
        cols_r[k + 1], cols_i[k + 1] = -scale * v_r, -scale * v_i
    return cols_r, cols_i


def total(terms):
    while len(terms) > 1:
        terms = [
            terms[i] + terms[i + 1] if i + 1 < len(terms) else terms[i]
            for i in range(0, len(terms), 2)
        ]
    return terms[0]


def combine(left_r, left_i, right_r, right_i):
    real = total([a * c - b * d for a, b, c, d in zip(left_r, left_i, right_r, right_i)])
    imag = total([a * d + b * c for a, b, c, d in zip(left_r, left_i, right_r, right_i)])
    return real, imag


def invert(ref):
    size = ref.shape[-1]
    shape = (SUB, size)
    lanes = lax.broadcasted_iota(jnp.int32, shape, 1)
    rows = lax.broadcasted_iota(jnp.int32, shape, 0)
    subs = PANEL // SUB

    def turn(value):
        return pltpu.roll(value, size - PANEL, 1)

    def step(p, carry):
        first = p * PANEL
        strips = []
        for j in range(subs):
            at = pl.ds(pl.multiple_of(first + j * SUB, SUB), SUB)
            strips.append((ref[0, at, :], ref[1, at, :]))
        opening = strips[0]
        strips = [(turn(strip[0]), turn(strip[1])) for strip in strips]
        for s in range(subs):
            start = size - PANEL + s * SUB
            inside = jnp.logical_and(lanes >= start, lanes < start + SUB)
            x_r, x_i = strips[s]
            if s == 0:
                p_r, p_i = pivot_inverse(opening[0], opening[1], 0)
            else:
                p_r, p_i = pivot_inverse(x_r, x_i, start)
            a_r = jnp.where(inside, (lanes - start == rows).astype(jnp.float32), x_r)
            a_i = jnp.where(inside, 0.0, x_i)
            r_r, r_i = combine(
                p_r, p_i, [down(a_r, c) for c in range(SUB)], [down(a_i, c) for c in range(SUB)]
            )
            b_r = [down(r_r, c) for c in range(SUB)]
            b_i = [down(r_i, c) for c in range(SUB)]
            for t in range(1, subs):
                j = (s + t) % subs
                x_r, x_i = strips[j]
                d_r, d_i = combine(
                    [across(x_r, start + c) for c in range(SUB)],
                    [across(x_i, start + c) for c in range(SUB)],
                    b_r,
                    b_i,
                )
                strips[j] = (jnp.where(inside, 0.0, x_r) - d_r, jnp.where(inside, 0.0, x_i) - d_i)
            strips[s] = (r_r, r_i)
        p_r = jnp.concatenate([strip[0] for strip in strips], axis=0)
        p_i = jnp.concatenate([strip[1] for strip in strips], axis=0)
        m_r, m_i = ref[0], ref[1]
        change = narrow_product(
            jnp.concatenate([m_r[:, :PANEL], m_i[:, :PANEL]], axis=1),
            jnp.concatenate(
                [jnp.concatenate([p_r, p_i], axis=1), jnp.concatenate([-p_i, p_r], axis=1)], axis=0
            ),
        )
        beyond = lax.broadcasted_iota(jnp.int32, (size, size), 1) >= PANEL
        ref[0] = turn(jnp.where(beyond, m_r, 0.0)) - change[:, :size]
        ref[1] = turn(jnp.where(beyond, m_i, 0.0)) - change[:, size:]
        at = pl.ds(pl.multiple_of(first, PANEL), PANEL)
        ref[0, at, :] = p_r
        ref[1, at, :] = p_i
        return carry

    lax.fori_loop(0, size // PANEL, step, 0)


def kernel(
    groups, chains, onsite_in, coupling_in, retained_in, out, onsite, coupling, retained,
    base, work, toward, left, prev, sigma_in, green_in, sigma_out, picked, table, received,
    u_send, u_recv, s_send, s_recv, g_send, g_recv, a_send, a_recv, fetch, hot,
    core, ship, right, c_send, c_recv,
):
    size = onsite.shape[-1]
    me = lax.axis_index("energy")
    pos = lax.axis_index("chain")
    half = chains // 2
    in_left = pos < half
    depth = jnp.where(in_left, pos, chains - 1 - pos)
    inner = jnp.where(in_left, pos + 1, pos - 1)
    outer = jnp.where(in_left, pos - 1, pos + 1)
    middle = depth == half - 1
    at_edge = depth == 0

    get_onsite = pltpu.make_async_copy(onsite_in, onsite, fetch.at[0])
    get_coupling = pltpu.make_async_copy(coupling_in, coupling, fetch.at[1])
    get_retained = pltpu.make_async_copy(retained_in, retained, fetch.at[2])
    get_onsite.start()
    get_coupling.start()
    get_retained.start()

    barrier = pltpu.get_barrier_semaphore()

    def greet(energy, chain):
        pl.semaphore_signal(barrier, inc=1, device_id=(energy, chain), device_id_type=MESH)

    for t in range(1, groups):
        greet(lax.rem(me + t, groups), pos)
    greet(me, inner)

    @pl.when(jnp.logical_not(at_edge))
    def _():
        greet(me, outer)

    def copy(src, dst, send, recv, energy, chain):
        return pltpu.make_async_remote_copy(
            src_ref=src, dst_ref=dst, send_sem=send, recv_sem=recv,
            device_id=(energy, chain), device_id_type=MESH,
        )

    coupling_copy = copy(coupling, prev, u_send, u_recv, me, lax.rem(pos + 1, chains))
    slot = jnp.where(middle, 1, 0)
    strip = size // CHUNKS
    beyond = jnp.clip(outer, 0, chains - 1)

    def part(ref, c):
        return ref.at[:, pl.ds(c * strip, strip), :]

    def sigma_copy(which, c):
        return copy(
            part(sigma_out, c), part(sigma_in.at[which], c), s_send.at[c], s_recv.at[which, c],
            me, inner,
        )

    def core_copy(c):
        return copy(part(ship, c), part(core, c), c_send.at[c], c_recv.at[c], me, beyond)

    if half > 2:
        green_copy = copy(work, green_in, g_send, g_recv, me, beyond)
    near = depth == half - 2
    passes_on = jnp.logical_and(jnp.logical_not(at_edge), jnp.logical_not(middle))

    get_onsite.wait()
    diagonal = (
        lax.broadcasted_iota(jnp.int32, (size, size), 0)
        == lax.broadcasted_iota(jnp.int32, (size, size), 1)
    ).astype(jnp.float32)
    energy = -2.0 + 4.0 * me.astype(jnp.float32) / groups
    base[0] = energy * diagonal - 0.5 * (onsite[0] + onsite[0].T)
    base[1] = BROADENING * diagonal - 0.5 * (onsite[1] - onsite[1].T)

    get_coupling.wait()

    @pl.when(pos == chains - 1)
    def _():
        coupler = load(coupling)
        square = product(coupler, adjoint(coupler))
        base[0] = base[0] - 0.5 * square[1]
        base[1] = base[1] + 0.5 * square[0]

    @pl.when(jnp.logical_not(at_edge))
    def _():
        pl.semaphore_wait(barrier, groups + 1)


    sends_coupling = jnp.logical_and(pos >= half - 1, pos < chains - 1)

    @pl.when(sends_coupling)
    def _():
        coupling_copy.start()

    columns = retained.shape[-1]
    across_rows = columns // 128

    def prepare():
        get_retained.wait()
        spot = lax.broadcasted_iota(jnp.int32, (size, columns), 0)

        def fill(group, carry):
            one = (spot == retained[group] % size).astype(jnp.float32).astype(jnp.bfloat16)
            hot[group, pl.ds(0, size), :] = one
            hot[group, pl.ds(size, size), :] = one
            return carry

        lax.fori_loop(0, groups, fill, 0)

    @pl.when(jnp.logical_not(at_edge))
    def _():
        prepare()
        for c in range(CHUNKS):
            sigma_copy(0, c).wait_recv()
        base[...] = base[...] - sigma_in[0]

    work[...] = base[...]
    invert(work)

    @pl.when(in_left)
    def _():
        toward[...] = coupling[...]

    @pl.when(jnp.logical_not(in_left))
    def _():
        coupling_copy.wait_recv()
        store(toward, adjoint(load(prev)))

    store(left, product(load(work), load(toward)))
    store(sigma_out, product(adjoint(load(toward)), load(left)))

    @pl.when(at_edge)
    def _():
        pl.semaphore_wait(barrier, groups)

    for c in range(CHUNKS):
        sigma_copy(slot, c).start()

    @pl.when(at_edge)
    def _():
        prepare()

    @pl.when(middle)
    def _():
        for c in range(CHUNKS):
            sigma_copy(1, c).wait_recv()
            at = pl.ds(c * strip, strip)
            last = base[:, at, :] - sigma_in[1, :, at, :]
            ship[:, at, :] = last
            core_copy(c).start()
            core[:, at, :] = last

    @pl.when(jnp.logical_not(middle))
    def _():
        store(right, product(adjoint(load(toward)), load(work)))

    def add_change(following):
        change = product(product(load(left), load(following), False), load(right), False)
        work[0] = work[0] + change[0]
        work[1] = work[1] + change[1]

    @pl.when(near)
    def _():
        for c in range(CHUNKS):
            core_copy(c).wait_recv()

    @pl.when(jnp.logical_or(middle, near))
    def _():
        invert(core)

    @pl.when(middle)
    def _():
        work[...] = core[...]

    @pl.when(near)
    def _():
        add_change(core)

    if half > 2:
        @pl.when(depth < half - 2)
        def _():
            green_copy.wait_recv()
            add_change(green_in)

        @pl.when(passes_on)
        def _():
            green_copy.start()

    full = load(work)
    planes = jnp.concatenate([full[0], full[1], full[0].T, full[1].T], axis=0)
    high = planes.astype(jnp.bfloat16)
    low = (planes - high.astype(jnp.float32)).astype(jnp.bfloat16)
    table[...] = jnp.concatenate([high, low], axis=1)

    def pick(group, target, place):
        chosen = retained[group]
        spot = lax.broadcasted_iota(jnp.int32, (size, columns), 0)
        keep = spot == chosen // size
        rows = jnp.dot(table[...], hot[group], preferred_element_type=jnp.float32)
        for p in range(4):
            part = jnp.where(keep, rows[p * size : (p + 1) * size], 0.0)
            line = jnp.sum(part, axis=0, keepdims=True)
            for r in range(across_rows):
                target[place, p, r : r + 1, :] = line[:, r * 128 : (r + 1) * 128]

    def exchange(t):
        peer = lax.rem(me + t, groups)
        return copy(
            picked.at[peer], received.at[me], a_send.at[peer], a_recv.at[me], peer, pos
        )

    def send_step(t, carry):
        peer = lax.rem(me + t, groups)
        pick(peer, picked, peer)
        exchange(t).start()
        return carry

    lax.fori_loop(1, groups, send_step, 0)
    pick(me, received, me)

    def arrive_step(t, carry):
        source = lax.rem(me + t, groups)
        copy(
            picked.at[source], received.at[source], a_send.at[source], a_recv.at[source],
            source, pos,
        ).wait_recv()
        return carry

    lax.fori_loop(1, groups, arrive_step, 0)

    def shift_step(w, carry):
        real = jnp.zeros(out.shape[2:], jnp.float32)
        imag = jnp.zeros(out.shape[2:], jnp.float32)
        for n in range(groups):
            other = lax.rem(w + n, groups)
            a_r, a_i = received[n, 0], received[n, 1]
            b_r, b_i = received[other, 2], received[other, 3]
            real = real + (a_r * b_r - a_i * b_i)
            imag = imag + (a_r * b_i + a_i * b_r)
        out[0, w] = real
        out[1, w] = imag
        return carry

    lax.fori_loop(0, groups, shift_step, 0)

    for c in range(CHUNKS):
        sigma_copy(slot, c).wait_send()

    @pl.when(middle)
    def _():
        for c in range(CHUNKS):
            core_copy(c).wait_send()

    @pl.when(sends_coupling)
    def _():
        coupling_copy.wait_send()

    if half > 2:
        @pl.when(passes_on)
        def _():
            green_copy.wait_send()

    def leave_step(t, carry):
        exchange(t).wait_send()
        return carry

    lax.fori_loop(1, groups, leave_step, 0)


def shards(onsite, coupling, retained):
    size = onsite.shape[-1]
    groups = lax.axis_size("energy")
    chains = lax.axis_size("chain")
    columns = retained.shape[-1] // groups
    block = pltpu.VMEM((2, size, size), jnp.float32)
    picks = pltpu.VMEM((groups, 4, columns // 128, 128), jnp.float32)
    dma = pltpu.SemaphoreType.DMA
    result = pl.pallas_call(
        functools.partial(kernel, groups, chains),
        out_shape=pltpu.VMEM((2, groups, columns // 128, 128), jnp.float32),
        in_specs=[pl.BlockSpec(memory_space=pltpu.HBM)] * 3,
        out_specs=pl.BlockSpec(memory_space=pltpu.VMEM),
        scratch_shapes=[
            block, block, pltpu.VMEM((groups, 1, columns), jnp.int32),
            block, block, block, block, block,
            pltpu.VMEM((2, 2, size, size), jnp.float32), block, block,
            picks,
            pltpu.VMEM((4 * size, 2 * size), jnp.bfloat16),
            picks,
            dma(()), dma(()), dma((CHUNKS,)), dma((2, CHUNKS)), dma(()), dma(()),
            dma((groups,)), dma((groups,)), dma((3,)),
            pltpu.VMEM((groups, 2 * size, columns), jnp.bfloat16),
            block, block, block, dma((CHUNKS,)), dma((CHUNKS,)),
        ],
        compiler_params=pltpu.CompilerParams(
            collective_id=0, has_side_effects=True, vmem_limit_bytes=GRANT
        ),
    )(onsite[0], coupling[0], retained.reshape(groups, 1, columns))
    return result.reshape(2, groups, 1, columns)


def solution(mesh):
    in_specs = (P("chain", None, None, None), P("chain", None, None, None), P("chain", None))
    out_specs = P(None, None, "chain", "energy")
    return jax.shard_map(shards, mesh=mesh, in_specs=in_specs, out_specs=out_specs, check_vma=False)
```

```python
import functools

import jax
import jax.numpy as jnp
from jax import lax
from jax.experimental import pallas as pl
from jax.experimental.pallas import tpu as pltpu
from jax.sharding import PartitionSpec as P

MESH = pl.DeviceIdType.MESH
SUB = 8
PANEL = 64
CHUNKS = 4
GRANT = 64 * 1024 * 1024 - 256 * 1024
BROADENING = 0.04


def product(left, right, exact=True):
    wide = jnp.concatenate(left, axis=1)
    real, imag = right
    tall = jnp.concatenate(
        [jnp.concatenate([real, imag], axis=1), jnp.concatenate([-imag, real], axis=1)], axis=0
    )
    if exact:
        both = jnp.dot(
            wide, tall, precision=lax.Precision.HIGHEST, preferred_element_type=jnp.float32
        )
    else:
        w0, w1 = split(wide, 2)
        t0, t1 = split(tall, 2)
        dot = functools.partial(jnp.dot, preferred_element_type=jnp.float32)
        both = dot(w0, t0) + (dot(w0, t1) + dot(w1, t0))
    size = real.shape[1]
    return both[:, :size], both[:, size:]


def adjoint(value):
    return value[0].T, -value[1].T


def load(ref):
    return ref[0], ref[1]


def store(ref, value):
    ref[0] = value[0]
    ref[1] = value[1]


def across(value, column):
    return jnp.broadcast_to(value[:, column : column + 1], value.shape)


def down(value, row):
    return jnp.broadcast_to(value[row : row + 1, :], value.shape)


def split(value, terms):
    pieces = []
    for _ in range(terms):
        piece = value.astype(jnp.bfloat16)
        pieces.append(piece)
        value = value - piece.astype(jnp.float32)
    return pieces


def narrow_product(left, right):
    l0, l1, l2 = split(left, 3)
    r0, r1, r2 = split(right, 3)
    small = jnp.dot(
        jnp.concatenate([l0, l2], axis=1),
        jnp.concatenate([r2, r0], axis=0),
        preferred_element_type=jnp.float32,
    )
    large = jnp.dot(
        jnp.concatenate([l0, l0, l1, l1], axis=1),
        jnp.concatenate([r0, r1, r0, r1], axis=0),
        preferred_element_type=jnp.float32,
    )
    return large + small


def reciprocal(value):
    guess = pl.reciprocal(value, approx=True)
    return guess * (2.0 - value * guess)


def pivot_inverse(real, imag, start):
    rows = lax.broadcasted_iota(jnp.int32, real.shape, 0)
    cols_r = [across(real, start + c) for c in range(SUB)]
    cols_i = [across(imag, start + c) for c in range(SUB)]
    for k in range(0, SUB, 2):
        a_r, a_i = down(cols_r[k], k), down(cols_i[k], k)
        b_r, b_i = down(cols_r[k + 1], k), down(cols_i[k + 1], k)
        c_r, c_i = down(cols_r[k], k + 1), down(cols_i[k], k + 1)
        d_r, d_i = down(cols_r[k + 1], k + 1), down(cols_i[k + 1], k + 1)
        det_r = (a_r * d_r - a_i * d_i) - (b_r * c_r - b_i * c_i)
        det_i = (a_r * d_i + a_i * d_r) - (b_r * c_i + b_i * c_r)
        scale = reciprocal(det_r * det_r + det_i * det_i)
        one, two = rows == k, rows == k + 1
        either = jnp.logical_or(one, two)
        e_r = jnp.where(one, -1.0, jnp.where(two, 0.0, cols_r[k]))
        e_i = jnp.where(either, 0.0, cols_i[k])
        f_r = jnp.where(two, -1.0, jnp.where(one, 0.0, cols_r[k + 1]))
        f_i = jnp.where(either, 0.0, cols_i[k + 1])
        u_r = (e_r * d_r - e_i * d_i) - (f_r * c_r - f_i * c_i)
        u_i = (e_r * d_i + e_i * d_r) - (f_r * c_i + f_i * c_r)
        v_r = (f_r * a_r - f_i * a_i) - (e_r * b_r - e_i * b_i)
        v_i = (f_r * a_i + f_i * a_r) - (e_r * b_i + e_i * b_r)
        u_r, u_i = u_r * det_r + u_i * det_i, u_i * det_r - u_r * det_i
        v_r, v_i = v_r * det_r + v_i * det_i, v_i * det_r - v_r * det_i
        for c in range(SUB):
            if c in (k, k + 1):
                continue
            m_r, m_i = down(cols_r[c], k), down(cols_i[c], k)
            n_r, n_i = down(cols_r[c], k + 1), down(cols_i[c], k + 1)
            w_r = (u_r * m_r - u_i * m_i) + (v_r * n_r - v_i * n_i)
            w_i = (u_r * m_i + u_i * m_r) + (v_r * n_i + v_i * n_r)
            cols_r[c] = jnp.where(either, 0.0, cols_r[c]) - scale * w_r
            cols_i[c] = jnp.where(either, 0.0, cols_i[c]) - scale * w_i
        cols_r[k], cols_i[k] = -scale * u_r, -scale * u_i
        cols_r[k + 1], cols_i[k + 1] = -scale * v_r, -scale * v_i
    return cols_r, cols_i


def total(terms):
    while len(terms) > 1:
        terms = [
            terms[i] + terms[i + 1] if i + 1 < len(terms) else terms[i]
            for i in range(0, len(terms), 2)
        ]
    return terms[0]


def combine(left_r, left_i, right_r, right_i):
    real = total([a * c - b * d for a, b, c, d in zip(left_r, left_i, right_r, right_i)])
    imag = total([a * d + b * c for a, b, c, d in zip(left_r, left_i, right_r, right_i)])
    return real, imag


def invert(ref):
    size = ref.shape[-1]
    shape = (SUB, size)
    lanes = lax.broadcasted_iota(jnp.int32, shape, 1)
    rows = lax.broadcasted_iota(jnp.int32, shape, 0)
    subs = PANEL // SUB

    def turn(value):
        return pltpu.roll(value, size - PANEL, 1)

    def step(p, carry):
        first = p * PANEL
        strips = []
        for j in range(subs):
            at = pl.ds(pl.multiple_of(first + j * SUB, SUB), SUB)
            strips.append((ref[0, at, :], ref[1, at, :]))
        opening = strips[0]
        strips = [(turn(strip[0]), turn(strip[1])) for strip in strips]
        for s in range(subs):
            start = size - PANEL + s * SUB
            inside = jnp.logical_and(lanes >= start, lanes < start + SUB)
            x_r, x_i = strips[s]
            if s == 0:
                p_r, p_i = pivot_inverse(opening[0], opening[1], 0)
            else:
                p_r, p_i = pivot_inverse(x_r, x_i, start)
            a_r = jnp.where(inside, (lanes - start == rows).astype(jnp.float32), x_r)
            a_i = jnp.where(inside, 0.0, x_i)
            r_r, r_i = combine(
                p_r, p_i, [down(a_r, c) for c in range(SUB)], [down(a_i, c) for c in range(SUB)]
            )
            b_r = [down(r_r, c) for c in range(SUB)]
            b_i = [down(r_i, c) for c in range(SUB)]
            for t in range(1, subs):
                j = (s + t) % subs
                x_r, x_i = strips[j]
                d_r, d_i = combine(
                    [across(x_r, start + c) for c in range(SUB)],
                    [across(x_i, start + c) for c in range(SUB)],
                    b_r,
                    b_i,
                )
                strips[j] = (jnp.where(inside, 0.0, x_r) - d_r, jnp.where(inside, 0.0, x_i) - d_i)
            strips[s] = (r_r, r_i)
        p_r = jnp.concatenate([strip[0] for strip in strips], axis=0)
        p_i = jnp.concatenate([strip[1] for strip in strips], axis=0)
        m_r, m_i = ref[0], ref[1]
        change = narrow_product(
            jnp.concatenate([m_r[:, :PANEL], m_i[:, :PANEL]], axis=1),
            jnp.concatenate(
                [jnp.concatenate([p_r, p_i], axis=1), jnp.concatenate([-p_i, p_r], axis=1)], axis=0
            ),
        )
        beyond = lax.broadcasted_iota(jnp.int32, (size, size), 1) >= PANEL
        ref[0] = turn(jnp.where(beyond, m_r, 0.0)) - change[:, :size]
        ref[1] = turn(jnp.where(beyond, m_i, 0.0)) - change[:, size:]
        at = pl.ds(pl.multiple_of(first, PANEL), PANEL)
        ref[0, at, :] = p_r
        ref[1, at, :] = p_i
        return carry

    lax.fori_loop(0, size // PANEL, step, 0)


def kernel(
    groups, chains, onsite_in, coupling_in, retained_in, out, onsite, coupling, retained,
    base, work, toward, left, prev, sigma_in, green_in, sigma_out, picked, table, received,
    u_send, u_recv, s_send, s_recv, g_send, g_recv, a_send, a_recv, fetch, hot,
    core, ship, right, c_send, c_recv, landing,
):
    size = onsite.shape[-1]
    me = lax.axis_index("energy")
    pos = lax.axis_index("chain")
    half = chains // 2
    in_left = pos < half
    depth = jnp.where(in_left, pos, chains - 1 - pos)
    inner = jnp.where(in_left, pos + 1, pos - 1)
    outer = jnp.where(in_left, pos - 1, pos + 1)
    middle = depth == half - 1
    at_edge = depth == 0

    get_onsite = pltpu.make_async_copy(onsite_in, onsite, fetch.at[0])
    get_coupling = pltpu.make_async_copy(coupling_in, coupling, fetch.at[1])
    get_retained = pltpu.make_async_copy(retained_in, retained, fetch.at[2])
    get_onsite.start()
    get_coupling.start()
    get_retained.start()

    barrier = pltpu.get_barrier_semaphore()

    def greet(energy, chain):
        pl.semaphore_signal(barrier, inc=1, device_id=(energy, chain), device_id_type=MESH)

    for t in range(1, groups):
        greet(lax.rem(me + t, groups), pos)
    greet(me, inner)

    @pl.when(jnp.logical_not(at_edge))
    def _():
        greet(me, outer)

    def copy(src, dst, send, recv, energy, chain):
        return pltpu.make_async_remote_copy(
            src_ref=src, dst_ref=dst, send_sem=send, recv_sem=recv,
            device_id=(energy, chain), device_id_type=MESH,
        )

    coupling_copy = copy(coupling, prev, u_send, u_recv, me, lax.rem(pos + 1, chains))
    slot = jnp.where(middle, 1, 0)
    strip = size // CHUNKS
    beyond = jnp.clip(outer, 0, chains - 1)

    def part(ref, c):
        return ref.at[:, pl.ds(c * strip, strip), :]

    def sigma_copy(which, c):
        return copy(
            part(sigma_out, c), part(sigma_in.at[which], c), s_send.at[c], s_recv.at[which, c],
            me, inner,
        )

    def core_copy(c):
        return copy(part(ship, c), part(landing, c), c_send.at[c], c_recv.at[c], me, beyond)

    if half > 2:
        green_copy = copy(work, green_in, g_send, g_recv, me, beyond)
    near = depth == half - 2
    passes_on = jnp.logical_and(jnp.logical_not(at_edge), jnp.logical_not(middle))

    get_onsite.wait()
    diagonal = (
        lax.broadcasted_iota(jnp.int32, (size, size), 0)
        == lax.broadcasted_iota(jnp.int32, (size, size), 1)
    ).astype(jnp.float32)
    energy = -2.0 + 4.0 * me.astype(jnp.float32) / groups
    base[0] = energy * diagonal - 0.5 * (onsite[0] + onsite[0].T)
    base[1] = BROADENING * diagonal - 0.5 * (onsite[1] - onsite[1].T)

    get_coupling.wait()

    @pl.when(pos == chains - 1)
    def _():
        coupler = load(coupling)
        square = product(coupler, adjoint(coupler))
        base[0] = base[0] - 0.5 * square[1]
        base[1] = base[1] + 0.5 * square[0]

    @pl.when(jnp.logical_not(at_edge))
    def _():
        pl.semaphore_wait(barrier, groups + 1)


    sends_coupling = jnp.logical_and(pos >= half - 1, pos < chains - 1)

    @pl.when(sends_coupling)
    def _():
        coupling_copy.start()

    columns = retained.shape[-1]
    across_rows = columns // 128

    def prepare():
        get_retained.wait()
        spot = lax.broadcasted_iota(jnp.int32, (size, columns), 0)

        def fill(group, carry):
            one = (spot == retained[group] % size).astype(jnp.float32).astype(jnp.bfloat16)
            hot[group, pl.ds(0, size), :] = one
            hot[group, pl.ds(size, size), :] = one
            return carry

        lax.fori_loop(0, groups, fill, 0)

    @pl.when(jnp.logical_not(at_edge))
    def _():
        prepare()
        for c in range(CHUNKS):
            sigma_copy(0, c).wait_recv()
        base[...] = base[...] - sigma_in[0]

    def add_change(following):
        change = product(product(load(left), load(following), False), load(right), False)
        work[0] = work[0] + change[0]
        work[1] = work[1] + change[1]

    def first_round():
        work[...] = core[...]

        @pl.when(in_left)
        def _():
            toward[...] = coupling[...]

        @pl.when(jnp.logical_not(in_left))
        def _():
            coupling_copy.wait_recv()
            store(toward, adjoint(load(prev)))

        store(left, product(load(work), load(toward)))
        store(sigma_out, product(adjoint(load(toward)), load(left)))

        @pl.when(at_edge)
        def _():
            pl.semaphore_wait(barrier, groups)

        for c in range(CHUNKS):
            sigma_copy(slot, c).start()

        @pl.when(at_edge)
        def _():
            prepare()

        @pl.when(middle)
        def _():
            for c in range(CHUNKS):
                sigma_copy(1, c).wait_recv()
                at = pl.ds(c * strip, strip)
                last = base[:, at, :] - sigma_in[1, :, at, :]
                ship[:, at, :] = last
                core_copy(c).start()
                core[:, at, :] = last

        @pl.when(jnp.logical_not(middle))
        def _():
            store(right, product(adjoint(load(toward)), load(work)))

        @pl.when(near)
        def _():
            for c in range(CHUNKS):
                core_copy(c).wait_recv()
            core[...] = landing[...]


    core[...] = base[...]

    def round_step(index, carry):
        first = index == 0

        @pl.when(jnp.logical_or(first, jnp.logical_or(middle, near)))
        def _():
            invert(core)

        @pl.when(first)
        def _():
            first_round()

        return carry

    lax.fori_loop(0, 2, round_step, 0)

    @pl.when(middle)
    def _():
        work[...] = core[...]

    @pl.when(near)
    def _():
        add_change(core)

    if half > 2:
        @pl.when(depth < half - 2)
        def _():
            green_copy.wait_recv()
            add_change(green_in)

        @pl.when(passes_on)
        def _():
            green_copy.start()

    full = load(work)
    planes = jnp.concatenate([full[0], full[1], full[0].T, full[1].T], axis=0)
    high = planes.astype(jnp.bfloat16)
    low = (planes - high.astype(jnp.float32)).astype(jnp.bfloat16)
    table[...] = jnp.concatenate([high, low], axis=1)

    def pick(group, target, place):
        chosen = retained[group]
        spot = lax.broadcasted_iota(jnp.int32, (size, columns), 0)
        keep = spot == chosen // size
        rows = jnp.dot(table[...], hot[group], preferred_element_type=jnp.float32)
        for p in range(4):
            part = jnp.where(keep, rows[p * size : (p + 1) * size], 0.0)
            line = jnp.sum(part, axis=0, keepdims=True)
            for r in range(across_rows):
                target[place, p, r : r + 1, :] = line[:, r * 128 : (r + 1) * 128]

    def exchange(t):
        peer = lax.rem(me + t, groups)
        return copy(
            picked.at[peer], received.at[me], a_send.at[peer], a_recv.at[me], peer, pos
        )

    def send_step(step, carry):
        peers = [lax.rem(me + 2 * step + 1 + t, groups) for t in range(2)]
        for peer in peers:
            pick(peer, picked, peer)
        exchange(2 * step + 1).start()

        @pl.when(step < groups // 2 - 1)
        def _():
            exchange(2 * step + 2).start()

        return carry

    lax.fori_loop(0, groups // 2, send_step, 0)
    received[me] = picked[me]

    def arrive_step(t, carry):
        source = lax.rem(me + t, groups)
        copy(
            picked.at[source], received.at[source], a_send.at[source], a_recv.at[source],
            source, pos,
        ).wait_recv()
        return carry

    lax.fori_loop(1, groups, arrive_step, 0)

    def shift_step(w, carry):
        real = jnp.zeros(out.shape[2:], jnp.float32)
        imag = jnp.zeros(out.shape[2:], jnp.float32)
        for n in range(groups):
            other = lax.rem(w + n, groups)
            a_r, a_i = received[n, 0], received[n, 1]
            b_r, b_i = received[other, 2], received[other, 3]
            real = real + (a_r * b_r - a_i * b_i)
            imag = imag + (a_r * b_i + a_i * b_r)
        out[0, w] = real
        out[1, w] = imag
        return carry

    lax.fori_loop(0, groups, shift_step, 0)

    for c in range(CHUNKS):
        sigma_copy(slot, c).wait_send()

    @pl.when(middle)
    def _():
        for c in range(CHUNKS):
            core_copy(c).wait_send()

    @pl.when(sends_coupling)
    def _():
        coupling_copy.wait_send()

    if half > 2:
        @pl.when(passes_on)
        def _():
            green_copy.wait_send()

    def leave_step(t, carry):
        exchange(t).wait_send()
        return carry

    lax.fori_loop(1, groups, leave_step, 0)


def shards(onsite, coupling, retained):
    size = onsite.shape[-1]
    groups = lax.axis_size("energy")
    chains = lax.axis_size("chain")
    columns = retained.shape[-1] // groups
    block = pltpu.VMEM((2, size, size), jnp.float32)
    picks = pltpu.VMEM((groups, 4, columns // 128, 128), jnp.float32)
    dma = pltpu.SemaphoreType.DMA
    result = pl.pallas_call(
        functools.partial(kernel, groups, chains),
        out_shape=pltpu.VMEM((2, groups, columns // 128, 128), jnp.float32),
        in_specs=[pl.BlockSpec(memory_space=pltpu.HBM)] * 3,
        out_specs=pl.BlockSpec(memory_space=pltpu.VMEM),
        scratch_shapes=[
            block, block, pltpu.VMEM((groups, 1, columns), jnp.int32),
            block, block, block, block, block,
            pltpu.VMEM((2, 2, size, size), jnp.float32), block, block,
            picks,
            pltpu.VMEM((4 * size, 2 * size), jnp.bfloat16),
            picks,
            dma(()), dma(()), dma((CHUNKS,)), dma((2, CHUNKS)), dma(()), dma(()),
            dma((groups,)), dma((groups,)), dma((3,)),
            pltpu.VMEM((groups, 2 * size, columns), jnp.bfloat16),
            block, block, block, dma((CHUNKS,)), dma((CHUNKS,)), block,
        ],
        compiler_params=pltpu.CompilerParams(
            collective_id=0, has_side_effects=True, vmem_limit_bytes=GRANT
        ),
    )(onsite[0], coupling[0], retained.reshape(groups, 1, columns))
    return result.reshape(2, groups, 1, columns)


def solution(mesh):
    in_specs = (P("chain", None, None, None), P("chain", None, None, None), P("chain", None))
    out_specs = P(None, None, "chain", "energy")
    return jax.shard_map(shards, mesh=mesh, in_specs=in_specs, out_specs=out_specs, check_vma=False)
```

```python
import functools

import jax
import jax.numpy as jnp
from jax import lax
from jax.experimental import pallas as pl
from jax.experimental.pallas import tpu as pltpu
from jax.sharding import PartitionSpec as P

MESH = pl.DeviceIdType.MESH
SUB = 8
PANEL = 64
CHUNKS = 4
GRANT = 64 * 1024 * 1024 - 256 * 1024
BROADENING = 0.04


def product(left, right, exact=False):
    wide = jnp.concatenate(left, axis=1)
    real, imag = right
    tall = jnp.concatenate(
        [jnp.concatenate([real, imag], axis=1), jnp.concatenate([-imag, real], axis=1)], axis=0
    )
    if exact:
        both = jnp.dot(
            wide, tall, precision=lax.Precision.HIGHEST, preferred_element_type=jnp.float32
        )
    else:
        w0, w1 = split(wide, 2)
        t0, t1 = split(tall, 2)
        dot = functools.partial(jnp.dot, preferred_element_type=jnp.float32)
        both = dot(w0, t0) + (dot(w0, t1) + dot(w1, t0))
    size = real.shape[1]
    return both[:, :size], both[:, size:]


def adjoint(value):
    return value[0].T, -value[1].T


def load(ref):
    return ref[0], ref[1]


def store(ref, value):
    ref[0] = value[0]
    ref[1] = value[1]


def across(value, column):
    return jnp.broadcast_to(value[:, column : column + 1], value.shape)


def down(value, row):
    return jnp.broadcast_to(value[row : row + 1, :], value.shape)


def split(value, terms):
    pieces = []
    for _ in range(terms):
        piece = value.astype(jnp.bfloat16)
        pieces.append(piece)
        value = value - piece.astype(jnp.float32)
    return pieces


def narrow_product(left, right):
    l0, l1, l2 = split(left, 3)
    r0, r1, r2 = split(right, 3)
    small = jnp.dot(
        jnp.concatenate([l0, l2], axis=1),
        jnp.concatenate([r2, r0], axis=0),
        preferred_element_type=jnp.float32,
    )
    large = jnp.dot(
        jnp.concatenate([l0, l0, l1, l1], axis=1),
        jnp.concatenate([r0, r1, r0, r1], axis=0),
        preferred_element_type=jnp.float32,
    )
    return large + small


def reciprocal(value):
    guess = pl.reciprocal(value, approx=True)
    return guess * (2.0 - value * guess)


def pivot_inverse(real, imag, start):
    rows = lax.broadcasted_iota(jnp.int32, real.shape, 0)
    cols_r = [across(real, start + c) for c in range(SUB)]
    cols_i = [across(imag, start + c) for c in range(SUB)]
    for k in range(0, SUB, 2):
        a_r, a_i = down(cols_r[k], k), down(cols_i[k], k)
        b_r, b_i = down(cols_r[k + 1], k), down(cols_i[k + 1], k)
        c_r, c_i = down(cols_r[k], k + 1), down(cols_i[k], k + 1)
        d_r, d_i = down(cols_r[k + 1], k + 1), down(cols_i[k + 1], k + 1)
        det_r = (a_r * d_r - a_i * d_i) - (b_r * c_r - b_i * c_i)
        det_i = (a_r * d_i + a_i * d_r) - (b_r * c_i + b_i * c_r)
        scale = reciprocal(det_r * det_r + det_i * det_i)
        one, two = rows == k, rows == k + 1
        either = jnp.logical_or(one, two)
        e_r = jnp.where(one, -1.0, jnp.where(two, 0.0, cols_r[k]))
        e_i = jnp.where(either, 0.0, cols_i[k])
        f_r = jnp.where(two, -1.0, jnp.where(one, 0.0, cols_r[k + 1]))
        f_i = jnp.where(either, 0.0, cols_i[k + 1])
        u_r = (e_r * d_r - e_i * d_i) - (f_r * c_r - f_i * c_i)
        u_i = (e_r * d_i + e_i * d_r) - (f_r * c_i + f_i * c_r)
        v_r = (f_r * a_r - f_i * a_i) - (e_r * b_r - e_i * b_i)
        v_i = (f_r * a_i + f_i * a_r) - (e_r * b_i + e_i * b_r)
        u_r, u_i = u_r * det_r + u_i * det_i, u_i * det_r - u_r * det_i
        v_r, v_i = v_r * det_r + v_i * det_i, v_i * det_r - v_r * det_i
        for c in range(SUB):
            if c in (k, k + 1):
                continue
            m_r, m_i = down(cols_r[c], k), down(cols_i[c], k)
            n_r, n_i = down(cols_r[c], k + 1), down(cols_i[c], k + 1)
            w_r = (u_r * m_r - u_i * m_i) + (v_r * n_r - v_i * n_i)
            w_i = (u_r * m_i + u_i * m_r) + (v_r * n_i + v_i * n_r)
            cols_r[c] = jnp.where(either, 0.0, cols_r[c]) - scale * w_r
            cols_i[c] = jnp.where(either, 0.0, cols_i[c]) - scale * w_i
        cols_r[k], cols_i[k] = -scale * u_r, -scale * u_i
        cols_r[k + 1], cols_i[k + 1] = -scale * v_r, -scale * v_i
    return cols_r, cols_i


def total(terms):
    while len(terms) > 1:
        terms = [
            terms[i] + terms[i + 1] if i + 1 < len(terms) else terms[i]
            for i in range(0, len(terms), 2)
        ]
    return terms[0]


def combine(left_r, left_i, right_r, right_i):
    real = total([a * c - b * d for a, b, c, d in zip(left_r, left_i, right_r, right_i)])
    imag = total([a * d + b * c for a, b, c, d in zip(left_r, left_i, right_r, right_i)])
    return real, imag


def invert(ref):
    size = ref.shape[-1]
    shape = (SUB, size)
    lanes = lax.broadcasted_iota(jnp.int32, shape, 1)
    rows = lax.broadcasted_iota(jnp.int32, shape, 0)
    subs = PANEL // SUB

    def turn(value):
        return pltpu.roll(value, size - PANEL, 1)

    def step(p, carry):
        first = p * PANEL
        strips = []
        for j in range(subs):
            at = pl.ds(pl.multiple_of(first + j * SUB, SUB), SUB)
            strips.append((ref[0, at, :], ref[1, at, :]))
        opening = strips[0]
        strips = [(turn(strip[0]), turn(strip[1])) for strip in strips]
        for s in range(subs):
            start = size - PANEL + s * SUB
            inside = jnp.logical_and(lanes >= start, lanes < start + SUB)
            x_r, x_i = strips[s]
            if s == 0:
                p_r, p_i = pivot_inverse(opening[0], opening[1], 0)
            else:
                p_r, p_i = pivot_inverse(x_r, x_i, start)
            a_r = jnp.where(inside, (lanes - start == rows).astype(jnp.float32), x_r)
            a_i = jnp.where(inside, 0.0, x_i)
            r_r, r_i = combine(
                p_r, p_i, [down(a_r, c) for c in range(SUB)], [down(a_i, c) for c in range(SUB)]
            )
            b_r = [down(r_r, c) for c in range(SUB)]
            b_i = [down(r_i, c) for c in range(SUB)]
            for t in range(1, subs):
                j = (s + t) % subs
                x_r, x_i = strips[j]
                d_r, d_i = combine(
                    [across(x_r, start + c) for c in range(SUB)],
                    [across(x_i, start + c) for c in range(SUB)],
                    b_r,
                    b_i,
                )
                strips[j] = (jnp.where(inside, 0.0, x_r) - d_r, jnp.where(inside, 0.0, x_i) - d_i)
            strips[s] = (r_r, r_i)
        p_r = jnp.concatenate([strip[0] for strip in strips], axis=0)
        p_i = jnp.concatenate([strip[1] for strip in strips], axis=0)
        m_r, m_i = ref[0], ref[1]
        change = narrow_product(
            jnp.concatenate([m_r[:, :PANEL], m_i[:, :PANEL]], axis=1),
            jnp.concatenate(
                [jnp.concatenate([p_r, p_i], axis=1), jnp.concatenate([-p_i, p_r], axis=1)], axis=0
            ),
        )
        beyond = lax.broadcasted_iota(jnp.int32, (size, size), 1) >= PANEL
        ref[0] = turn(jnp.where(beyond, m_r, 0.0)) - change[:, :size]
        ref[1] = turn(jnp.where(beyond, m_i, 0.0)) - change[:, size:]
        at = pl.ds(pl.multiple_of(first, PANEL), PANEL)
        ref[0, at, :] = p_r
        ref[1, at, :] = p_i
        return carry

    lax.fori_loop(0, size // PANEL, step, 0)


def kernel(
    groups, chains, onsite_in, coupling_in, retained_in, out, onsite, coupling, retained,
    base, work, toward, left, prev, sigma_in, green_in, sigma_out, picked, table, received,
    u_send, u_recv, s_send, s_recv, g_send, g_recv, a_send, a_recv, fetch, hot,
    core, ship, right, c_send, c_recv, landing,
):
    size = onsite.shape[-1]
    me = lax.axis_index("energy")
    pos = lax.axis_index("chain")
    half = chains // 2
    in_left = pos < half
    depth = jnp.where(in_left, pos, chains - 1 - pos)
    inner = jnp.where(in_left, pos + 1, pos - 1)
    outer = jnp.where(in_left, pos - 1, pos + 1)
    middle = depth == half - 1
    at_edge = depth == 0

    get_onsite = pltpu.make_async_copy(onsite_in, onsite, fetch.at[0])
    get_coupling = pltpu.make_async_copy(coupling_in, coupling, fetch.at[1])
    get_retained = pltpu.make_async_copy(retained_in, retained, fetch.at[2])
    get_onsite.start()
    get_coupling.start()
    get_retained.start()

    barrier = pltpu.get_barrier_semaphore()

    def greet(energy, chain):
        pl.semaphore_signal(barrier, inc=1, device_id=(energy, chain), device_id_type=MESH)

    for t in range(1, groups):
        greet(lax.rem(me + t, groups), pos)
    greet(me, inner)

    @pl.when(jnp.logical_not(at_edge))
    def _():
        greet(me, outer)

    def copy(src, dst, send, recv, energy, chain):
        return pltpu.make_async_remote_copy(
            src_ref=src, dst_ref=dst, send_sem=send, recv_sem=recv,
            device_id=(energy, chain), device_id_type=MESH,
        )

    coupling_copy = copy(coupling, prev, u_send, u_recv, me, lax.rem(pos + 1, chains))
    slot = jnp.where(middle, 1, 0)
    strip = size // CHUNKS
    beyond = jnp.clip(outer, 0, chains - 1)

    def part(ref, c):
        return ref.at[:, pl.ds(c * strip, strip), :]

    def sigma_copy(which, c):
        return copy(
            part(sigma_out, c), part(sigma_in.at[which], c), s_send.at[c], s_recv.at[which, c],
            me, inner,
        )

    def core_copy(c):
        return copy(part(ship, c), part(landing, c), c_send.at[c], c_recv.at[c], me, beyond)

    if half > 2:
        green_copy = copy(work, green_in, g_send, g_recv, me, beyond)
    near = depth == half - 2
    passes_on = jnp.logical_and(jnp.logical_not(at_edge), jnp.logical_not(middle))

    get_onsite.wait()
    diagonal = (
        lax.broadcasted_iota(jnp.int32, (size, size), 0)
        == lax.broadcasted_iota(jnp.int32, (size, size), 1)
    ).astype(jnp.float32)
    energy = -2.0 + 4.0 * me.astype(jnp.float32) / groups
    base[0] = energy * diagonal - 0.5 * (onsite[0] + onsite[0].T)
    base[1] = BROADENING * diagonal - 0.5 * (onsite[1] - onsite[1].T)

    get_coupling.wait()

    @pl.when(pos == chains - 1)
    def _():
        coupler = load(coupling)
        square = product(coupler, adjoint(coupler))
        base[0] = base[0] - 0.5 * square[1]
        base[1] = base[1] + 0.5 * square[0]

    @pl.when(jnp.logical_not(at_edge))
    def _():
        pl.semaphore_wait(barrier, groups + 1)


    sends_coupling = jnp.logical_and(pos >= half - 1, pos < chains - 1)

    @pl.when(sends_coupling)
    def _():
        coupling_copy.start()

    columns = retained.shape[-1]
    across_rows = columns // 128

    def prepare():
        get_retained.wait()
        spot = lax.broadcasted_iota(jnp.int32, (size, columns), 0)

        def fill(group, carry):
            one = (spot == retained[group] % size).astype(jnp.float32).astype(jnp.bfloat16)
            hot[group, pl.ds(0, size), :] = one
            hot[group, pl.ds(size, size), :] = one
            return carry

        lax.fori_loop(0, groups, fill, 0)

    @pl.when(jnp.logical_not(at_edge))
    def _():
        prepare()
        for c in range(CHUNKS):
            sigma_copy(0, c).wait_recv()
        base[...] = base[...] - sigma_in[0]

    def add_change(following):
        change = product(product(load(left), load(following), False), load(right), False)
        work[0] = work[0] + change[0]
        work[1] = work[1] + change[1]

    def first_round():
        work[...] = core[...]

        @pl.when(in_left)
        def _():
            toward[...] = coupling[...]

        @pl.when(jnp.logical_not(in_left))
        def _():
            coupling_copy.wait_recv()
            store(toward, adjoint(load(prev)))

        store(left, product(load(work), load(toward)))
        store(sigma_out, product(adjoint(load(toward)), load(left)))

        @pl.when(at_edge)
        def _():
            pl.semaphore_wait(barrier, groups)

        for c in range(CHUNKS):
            sigma_copy(slot, c).start()

        @pl.when(at_edge)
        def _():
            prepare()

        @pl.when(middle)
        def _():
            for c in range(CHUNKS):
                sigma_copy(1, c).wait_recv()
                at = pl.ds(c * strip, strip)
                last = base[:, at, :] - sigma_in[1, :, at, :]
                ship[:, at, :] = last
                core_copy(c).start()
                core[:, at, :] = last

        @pl.when(jnp.logical_not(middle))
        def _():
            store(right, product(adjoint(load(toward)), load(work)))

        @pl.when(near)
        def _():
            for c in range(CHUNKS):
                core_copy(c).wait_recv()
            core[...] = landing[...]


    core[...] = base[...]

    def round_step(index, carry):
        first = index == 0

        @pl.when(jnp.logical_or(first, jnp.logical_or(middle, near)))
        def _():
            invert(core)

        @pl.when(first)
        def _():
            first_round()

        return carry

    lax.fori_loop(0, 2, round_step, 0)

    @pl.when(middle)
    def _():
        work[...] = core[...]

    @pl.when(near)
    def _():
        add_change(core)

    if half > 2:
        @pl.when(depth < half - 2)
        def _():
            green_copy.wait_recv()
            add_change(green_in)

        @pl.when(passes_on)
        def _():
            green_copy.start()

    full = load(work)
    planes = jnp.concatenate([full[0], full[1], full[0].T, full[1].T], axis=0)
    high = planes.astype(jnp.bfloat16)
    low = (planes - high.astype(jnp.float32)).astype(jnp.bfloat16)
    table[...] = jnp.concatenate([high, low], axis=1)

    def pick(group, target, place):
        chosen = retained[group]
        spot = lax.broadcasted_iota(jnp.int32, (size, columns), 0)
        keep = spot == chosen // size
        rows = jnp.dot(table[...], hot[group], preferred_element_type=jnp.float32)
        for p in range(4):
            part = jnp.where(keep, rows[p * size : (p + 1) * size], 0.0)
            line = jnp.sum(part, axis=0, keepdims=True)
            for r in range(across_rows):
                target[place, p, r : r + 1, :] = line[:, r * 128 : (r + 1) * 128]

    def exchange(t):
        peer = lax.rem(me + t, groups)
        return copy(
            picked.at[peer], received.at[me], a_send.at[peer], a_recv.at[me], peer, pos
        )

    def send_step(step, carry):
        peers = [lax.rem(me + 2 * step + 1 + t, groups) for t in range(2)]
        for peer in peers:
            pick(peer, picked, peer)
        exchange(2 * step + 1).start()

        @pl.when(step < groups // 2 - 1)
        def _():
            exchange(2 * step + 2).start()

        return carry

    lax.fori_loop(0, groups // 2, send_step, 0)
    received[me] = picked[me]

    def arrive_step(t, carry):
        source = lax.rem(me + t, groups)
        copy(
            picked.at[source], received.at[source], a_send.at[source], a_recv.at[source],
            source, pos,
        ).wait_recv()
        return carry

    lax.fori_loop(1, groups, arrive_step, 0)

    def shift_step(w, carry):
        real = jnp.zeros(out.shape[2:], jnp.float32)
        imag = jnp.zeros(out.shape[2:], jnp.float32)
        for n in range(groups):
            other = lax.rem(w + n, groups)
            a_r, a_i = received[n, 0], received[n, 1]
            b_r, b_i = received[other, 2], received[other, 3]
            real = real + (a_r * b_r - a_i * b_i)
            imag = imag + (a_r * b_i + a_i * b_r)
        out[0, w] = real
        out[1, w] = imag
        return carry

    lax.fori_loop(0, groups, shift_step, 0)

    for c in range(CHUNKS):
        sigma_copy(slot, c).wait_send()

    @pl.when(middle)
    def _():
        for c in range(CHUNKS):
            core_copy(c).wait_send()

    @pl.when(sends_coupling)
    def _():
        coupling_copy.wait_send()

    if half > 2:
        @pl.when(passes_on)
        def _():
            green_copy.wait_send()

    def leave_step(t, carry):
        exchange(t).wait_send()
        return carry

    lax.fori_loop(1, groups, leave_step, 0)


def shards(onsite, coupling, retained):
    size = onsite.shape[-1]
    groups = lax.axis_size("energy")
    chains = lax.axis_size("chain")
    columns = retained.shape[-1] // groups
    block = pltpu.VMEM((2, size, size), jnp.float32)
    picks = pltpu.VMEM((groups, 4, columns // 128, 128), jnp.float32)
    dma = pltpu.SemaphoreType.DMA
    result = pl.pallas_call(
        functools.partial(kernel, groups, chains),
        out_shape=pltpu.VMEM((2, groups, columns // 128, 128), jnp.float32),
        in_specs=[pl.BlockSpec(memory_space=pltpu.HBM)] * 3,
        out_specs=pl.BlockSpec(memory_space=pltpu.VMEM),
        scratch_shapes=[
            block, block, pltpu.VMEM((groups, 1, columns), jnp.int32),
            block, block, block, block, block,
            pltpu.VMEM((2, 2, size, size), jnp.float32), block, block,
            picks,
            pltpu.VMEM((4 * size, 2 * size), jnp.bfloat16),
            picks,
            dma(()), dma(()), dma((CHUNKS,)), dma((2, CHUNKS)), dma(()), dma(()),
            dma((groups,)), dma((groups,)), dma((3,)),
            pltpu.VMEM((groups, 2 * size, columns), jnp.bfloat16),
            block, block, block, dma((CHUNKS,)), dma((CHUNKS,)), block,
        ],
        compiler_params=pltpu.CompilerParams(
            collective_id=0, has_side_effects=True, vmem_limit_bytes=GRANT
        ),
    )(onsite[0], coupling[0], retained.reshape(groups, 1, columns))
    return result.reshape(2, groups, 1, columns)


def solution(mesh):
    in_specs = (P("chain", None, None, None), P("chain", None, None, None), P("chain", None))
    out_specs = P(None, None, "chain", "energy")
    return jax.shard_map(shards, mesh=mesh, in_specs=in_specs, out_specs=out_specs, check_vma=False)
```
